32 devices in a mesh: dp: 4 (over y, x), tensor: 8 (over z, core).
Axes of the slice: x: 2, y: 2, z: 4, core: 2. Of those that a mesh axis runs over, the one named last changes fastest.
Arguments:
- prompt_states: bfloat16 [8, 512, 2048], P('dp', 'tensor')
- decode_states: bfloat16 [128, 2048], P(('dp', 'tensor'))
- cache: bfloat16 [2, 136, 384, 2048], P(None, 'dp', 'tensor'), may hold values from -160 to 160
- prompt_starts: int32 [8], replicated, may hold values from 0 to 384, as said below
- decode_lengths: int32 [128], replicated, may hold values from 1 to 384, as said below
- decode_slots: int32 [128], replicated, may hold values from 0 to 127, each once
- w_qkv: bfloat16 [3, 2048, 2048], P(None, None, 'tensor')
- w_out: bfloat16 [2048, 2048], P('tensor')
- w_gate_up: bfloat16 [2, 2048, 8192], P(None, None, 'tensor')
- w_down: bfloat16 [8192, 2048], P('tensor')
- gains: float32 [4, 2048], replicated, may hold values from 0.25 to 1.75
Outputs:
- prompt_out: bfloat16 [8, 512, 2048], P('dp', 'tensor')
- decode_out: bfloat16 [128, 2048], P(('dp', 'tensor'))
- new_prompt_kv: bfloat16 [2, 8, 512, 2048], P(None, 'dp', 'tensor')
- new_decode_kv: bfloat16 [2, 128, 2048], P(None, ('dp', 'tensor'))
The draws below stay inside these ranges and needn't reach their ends.
Inputs may be any that keep to these rules, and one draw needn't show every extreme that they name: Decode request e sits in decode slot decode_slots[e]; each slot holds one request. `prompt_starts`: some prompt has exactly 384 cached positions. `decode_lengths`: some decode request has exactly 384 cached positions.
All inputs are finite; a program needn't handle non-finite values.
Results may differ from the reference program's by a relative error of at most 0.02.
Values may be sent and summed in bfloat16 or wider, within the bound.
No kernel may reach another device: no remote copies, remote signals or barrier semaphores. Data moves between devices by JAX's collectives and lax.ppermute only.
A program may use at most 256 MiB of HBM per device.

```python
import jax
import jax.numpy as jnp
from jax import lax

D = 2048
HD = 128
FF = 8192
GROUP = 512
PRE_DEV = 2
DEC_DEV = 32
CTX_DEV = 48
SLOTS_DEV = 34
SLOTS = 136
PREFILLS = 8
DECODES = 128
CACHE = 384
N_TENSOR = 8


def scaled_weight(key, full_shape, fan_in):
    key_base, key_scale = jax.random.split(key)
    column_shape = full_shape[:-2] + (1, full_shape[-1])
    base_values = jnp.clip(jax.random.normal(key_base, full_shape, jnp.float32), -6.0, 6.0)
    column_scale = jnp.exp(jax.random.uniform(key_scale, column_shape, jnp.float32, 0.0, 2.3025851))
    return base_values * column_scale * fan_in ** (-0.5) / 4.6


def scaled_rows(key, full_shape):
    key_base, key_scale = jax.random.split(key)
    row_shape = full_shape[:-1] + (1,)
    base_values = jnp.clip(jax.random.normal(key_base, full_shape, jnp.float32), -6.0, 6.0)
    row_scale = jnp.exp(jax.random.uniform(key_scale, row_shape, jnp.float32, -1.2039728, 1.0986123))
    return base_values * row_scale


def skewed_lengths(key, count, lowest):
    key_first, key_second, key_pick = jax.random.split(key, 3)
    first_draw = jax.random.randint(key_first, (count,), lowest, CACHE + 1)
    second_draw = jax.random.randint(key_second, (count,), lowest, CACHE + 1)
    chosen = jax.random.randint(key_pick, (), 0, count)
    lengths = jnp.minimum(first_draw, second_draw)
    return jnp.where(jnp.arange(count) == chosen, CACHE, lengths).astype(jnp.int32)


def draw_prompt_states(key, part):
    return scaled_rows(key, (PREFILLS, GROUP, D)).astype(jnp.bfloat16)


def draw_decode_states(key, part):
    return scaled_rows(key, (DECODES, D)).astype(jnp.bfloat16)


def draw_cache(key, part):
    key_keys, key_values = jax.random.split(key, 2)
    full_shape = (SLOTS, CACHE, D)
    stored_keys = jnp.clip(jax.random.normal(key_keys, full_shape, jnp.float32), -6.0, 6.0)
    stored_values = jnp.clip(jax.random.normal(key_values, full_shape, jnp.float32), -6.0, 6.0)
    return jnp.stack([stored_keys, stored_values]).astype(jnp.bfloat16)


def draw_prompt_starts(key, part):
    return skewed_lengths(key, PREFILLS, 0)


def draw_decode_lengths(key, part):
    return skewed_lengths(key, DECODES, 1)


def draw_w_qkv(key, part):
    return scaled_weight(key, (3, D, D), D).astype(jnp.bfloat16)


def draw_w_out(key, part):
    return scaled_weight(key, (D, D), D).astype(jnp.bfloat16)


def draw_w_gate_up(key, part):
    return scaled_weight(key, (2, D, FF), D).astype(jnp.bfloat16)


def draw_w_down(key, part):
    return scaled_weight(key, (FF, D), FF).astype(jnp.bfloat16)


def setup_inputs(seed: int = 0) -> dict:
    key_list = jax.random.split(jax.random.key(seed), 12)
    prompt_states = draw_prompt_states(jax.random.fold_in(key_list[11], 71), 0)
    decode_states = draw_decode_states(jax.random.fold_in(key_list[11], 71), 0)
    cache = draw_cache(jax.random.fold_in(key_list[11], 71), 0)
    prompt_starts = draw_prompt_starts(jax.random.fold_in(key_list[11], 71), 0)
    decode_lengths = draw_decode_lengths(jax.random.fold_in(key_list[11], 71), 0)
    decode_slots = jax.random.permutation(key_list[5], DECODES).astype(jnp.int32)
    w_qkv = draw_w_qkv(jax.random.fold_in(key_list[11], 71), 0)
    w_out = draw_w_out(jax.random.fold_in(key_list[11], 71), 0)
    w_gate_up = draw_w_gate_up(jax.random.fold_in(key_list[11], 71), 0)
    w_down = draw_w_down(jax.random.fold_in(key_list[11], 71), 0)
    gains = jnp.clip(1.0 + 0.15 * jax.random.normal(key_list[10], (4, D), jnp.float32), 0.25, 1.75)
    return {"prompt_states": prompt_states, "decode_states": decode_states, "cache": cache, "prompt_starts": prompt_starts, "decode_lengths": decode_lengths, "decode_slots": decode_slots, "w_qkv": w_qkv, "w_out": w_out, "w_gate_up": w_gate_up, "w_down": w_down, "gains": gains}


EPSILON = 1e-06
ROPE_BASE = 500000.0
MASKED_SCORE = -1e+30

def rms_scale(values, gain_vec):
    return values * lax.rsqrt(lax.optimization_barrier(jnp.mean(values * values, axis=-1, keepdims=True)) + EPSILON) * gain_vec

def rotate(values, positions):
    full_shape = values.shape
    paired = values.reshape(full_shape[:-1] + (full_shape[-1] // HD, HD // 2, 2))
    freq_index = jnp.arange(HD // 2, dtype=jnp.float32)
    inv_freq = jnp.power(ROPE_BASE, -2.0 * freq_index / HD)
    angles = positions.astype(jnp.float32)[..., None, None] * inv_freq
    cosine = jnp.cos(angles)
    sine_values = jnp.sin(angles)
    even_part = paired[..., 0]
    odd_part = paired[..., 1]
    turned = jnp.stack([even_part * cosine - odd_part * sine_values, even_part * sine_values + odd_part * cosine], axis=-1)
    return turned.reshape(full_shape)

def round_trip(values):
    rounded = lax.optimization_barrier(values.astype(jnp.bfloat16))
    return rounded.astype(jnp.float32)

def block_sum(operand, weights, blocks):
    row_count = operand.shape[0]
    inner_width = operand.shape[1] // blocks
    operands = jnp.transpose(operand.reshape(row_count, blocks, inner_width), (1, 0, 2))
    weight_blocks = weights.reshape(blocks, inner_width, weights.shape[1])

    def accumulate(running, couple):
        partial_value = jnp.dot(couple[0], couple[1], preferred_element_type=jnp.float32).astype(jnp.bfloat16)
        partial_value = lax.optimization_barrier(partial_value)
        return (running + partial_value.astype(jnp.float32), None)
    initial = jnp.zeros((row_count, weights.shape[1]), jnp.float32)
    running, unused = lax.scan(accumulate, initial, (operands, weight_blocks))
    return running

def reference(prompt_states, decode_states, cache, prompt_starts, decode_lengths, decode_slots, w_qkv, w_out, w_gate_up, w_down, gains):
    head_count = D // HD
    prompt_rows = PREFILLS * GROUP
    part_rows = GROUP // N_TENSOR
    states = jnp.concatenate([prompt_states.reshape(prompt_rows, D), decode_states], axis=0)
    projected = jnp.einsum('rd,kde->kre', states.astype(jnp.float32), w_qkv.astype(jnp.float32), precision=lax.Precision.HIGHEST)
    query_raw = projected[0].astype(jnp.bfloat16)
    key_raw = projected[1].astype(jnp.bfloat16)
    value_new = projected[2].astype(jnp.bfloat16)
    slot_request = jnp.zeros((DECODES,), jnp.int32).at[decode_slots].set(jnp.arange(DECODES, dtype=jnp.int32))
    slot_length = decode_lengths[slot_request]
    offsets = jnp.arange(GROUP, dtype=jnp.int32)
    prompt_pos = prompt_starts[:, None] + offsets[None, :]
    positions = jnp.concatenate([prompt_pos.reshape(prompt_rows), slot_length], axis=0)
    query_new = rotate(rms_scale(query_raw.astype(jnp.float32), gains[0]), positions).astype(jnp.bfloat16)
    key_new = rotate(rms_scale(key_raw.astype(jnp.float32), gains[1]), positions).astype(jnp.bfloat16)
    scale_factor = HD ** (-0.5)
    prompt_ids = jnp.arange(PREFILLS, dtype=jnp.int32)
    prompt_cache = prompt_ids // PRE_DEV * SLOTS_DEV + prompt_ids % PRE_DEV
    decode_ids = jnp.arange(DECODES, dtype=jnp.int32)
    decode_cache = decode_ids // DEC_DEV * SLOTS_DEV + PRE_DEV + decode_ids % DEC_DEV
    decode_block = decode_ids % DEC_DEV // (DEC_DEV // N_TENSOR)
    cache_pos = jnp.arange(CACHE, dtype=jnp.int32)
    block_ids = jnp.arange(N_TENSOR, dtype=jnp.int32)

    def prompt_block(inputs):
        slot_index, start_pos, queries, keys_in, values_in = inputs
        cached_keys = cache[0, slot_index].reshape(CACHE, head_count, HD).astype(jnp.float32)
        cached_values = cache[1, slot_index].reshape(N_TENSOR, CTX_DEV, head_count, HD).astype(jnp.float32)
        all_keys = jnp.concatenate([cached_keys, keys_in.reshape(GROUP, head_count, HD).astype(jnp.float32)], axis=0)
        fresh_values = values_in.reshape(N_TENSOR, part_rows, head_count, HD).astype(jnp.float32)
        query_heads = queries.reshape(GROUP, head_count, HD).astype(jnp.float32)
        scores = jnp.einsum('ihe,jhe->hij', query_heads, all_keys, precision=lax.Precision.HIGHEST) * scale_factor
        live_mask = jnp.concatenate([jnp.broadcast_to((cache_pos < start_pos)[None, :], (GROUP, CACHE)), offsets[None, :] <= offsets[:, None]], axis=1)
        scores = jnp.where(live_mask[None], scores, MASKED_SCORE)
        highest = lax.optimization_barrier(jnp.max(scores, axis=-1, keepdims=True))
        weights = jnp.where(live_mask[None], jnp.exp(scores - highest), 0.0)
        totals = lax.optimization_barrier(jnp.sum(weights, axis=-1))
        probs = round_trip(weights)
        cached_probs = probs[..., :CACHE].reshape(head_count, GROUP, N_TENSOR, CTX_DEV)
        fresh_probs = probs[..., CACHE:].reshape(head_count, GROUP, N_TENSOR, part_rows)
        partials = jnp.einsum('hitj,tjhe->tihe', cached_probs, cached_values, precision=lax.Precision.HIGHEST)
        partials = partials + jnp.einsum('hitj,tjhe->tihe', fresh_probs, fresh_values, precision=lax.Precision.HIGHEST)
        mixed_sum = lax.optimization_barrier(jnp.sum(round_trip(partials), axis=0))
        return (mixed_sum / jnp.transpose(totals)[:, :, None]).reshape(GROUP, D).astype(jnp.bfloat16)

    def decode_one(inputs):
        slot_index, length, owner_block, query_row, key_own, value_own = inputs
        cached_keys = cache[0, slot_index].reshape(CACHE, head_count, HD).astype(jnp.float32)
        cached_values = cache[1, slot_index].reshape(N_TENSOR, CTX_DEV, head_count, HD).astype(jnp.float32)
        query_heads = query_row.reshape(head_count, HD).astype(jnp.float32)
        cached_scores = jnp.einsum('he,jhe->hj', query_heads, cached_keys, precision=lax.Precision.HIGHEST) * scale_factor
        own_score = lax.optimization_barrier(jnp.sum(query_heads * key_own.reshape(head_count, HD).astype(jnp.float32), axis=-1)) * scale_factor
        live_mask = cache_pos < length
        cached_scores = jnp.where(live_mask[None], cached_scores, MASKED_SCORE)
        highest = jnp.maximum(lax.optimization_barrier(jnp.max(cached_scores, axis=-1)), own_score)
        cached_weights = jnp.where(live_mask[None], jnp.exp(cached_scores - highest[:, None]), 0.0)
        own_weight = jnp.exp(own_score - highest)
        totals = lax.optimization_barrier(jnp.sum(cached_weights, axis=-1)) + own_weight
        cached_probs = round_trip(cached_weights).reshape(head_count, N_TENSOR, CTX_DEV)
        own_prob = round_trip(own_weight)
        partials = jnp.einsum('htj,tjhe->the', cached_probs, cached_values, precision=lax.Precision.HIGHEST)
        own_term = own_prob[:, None] * value_own.reshape(head_count, HD).astype(jnp.float32)
        pick = jnp.where(block_ids == owner_block, 1.0, 0.0).astype(jnp.float32)
        partials = partials + pick[:, None, None] * own_term[None]
        mixed_sum = lax.optimization_barrier(jnp.sum(round_trip(partials), axis=0))
        return (mixed_sum / totals[:, None]).reshape(D).astype(jnp.bfloat16)
    prompt_attn = lax.map(prompt_block, (prompt_cache, prompt_starts, query_new[:prompt_rows].reshape(PREFILLS, GROUP, D), key_new[:prompt_rows].reshape(PREFILLS, GROUP, D), value_new[:prompt_rows].reshape(PREFILLS, GROUP, D)))
    decode_attn = lax.map(decode_one, (decode_cache, slot_length, decode_block, query_new[prompt_rows:], key_new[prompt_rows:], value_new[prompt_rows:]))
    attended = jnp.concatenate([prompt_attn.reshape(prompt_rows, D), decode_attn], axis=0)
    attn_sum = block_sum(attended, w_out, N_TENSOR)
    hidden = (states.astype(jnp.float32) + rms_scale(attn_sum, gains[2])).astype(jnp.bfloat16)
    gate_up = jnp.einsum('rd,kdf->krf', hidden.astype(jnp.float32), w_gate_up.astype(jnp.float32), precision=lax.Precision.HIGHEST)
    activated = (jax.nn.silu(gate_up[0]) * gate_up[1]).astype(jnp.bfloat16)
    ffn_sum = block_sum(activated, w_down, N_TENSOR)
    output = (hidden.astype(jnp.float32) + rms_scale(ffn_sum, gains[3])).astype(jnp.bfloat16)
    prompt_out = output[:prompt_rows].reshape(PREFILLS, GROUP, D)
    decode_out = output[prompt_rows:][decode_slots]
    new_prompt_kv = jnp.stack([key_new[:prompt_rows], value_new[:prompt_rows]]).reshape(2, PREFILLS, GROUP, D)
    new_decode_kv = jnp.stack([key_new[prompt_rows:], value_new[prompt_rows:]])
    return (prompt_out, decode_out, new_prompt_kv, new_decode_kv)
```

```python
import jax
import jax.numpy as jnp
from jax import lax
from jax.experimental import pallas as pl
from jax.experimental.pallas import tpu as pltpu
from jax.sharding import PartitionSpec as P

HD = 128


EPSILON = 1e-06
ROPE_BASE = 500000.0
MASKED_SCORE = -1e30


def rms_scale(values, gain_vec):
    return (
        values * lax.rsqrt(jnp.mean(values * values, axis=-1, keepdims=True) + EPSILON) * gain_vec
    )


def rotate(values, positions):
    full_shape = values.shape
    paired = values.reshape(full_shape[:-1] + (full_shape[-1] // HD, HD // 2, 2))
    freq_index = jnp.arange(HD // 2, dtype=jnp.float32)
    inv_freq = jnp.power(ROPE_BASE, -2.0 * freq_index / HD)
    angles = positions.astype(jnp.float32)[..., None, None] * inv_freq
    cosine = jnp.cos(angles)
    sine_values = jnp.sin(angles)
    even_part = paired[..., 0]
    odd_part = paired[..., 1]
    turned = jnp.stack(
        [even_part * cosine - odd_part * sine_values, even_part * sine_values + odd_part * cosine],
        axis=-1,
    )
    return turned.reshape(full_shape)


def split_rows(stacked, tensors, pre_dev, part_rows):
    tail_shape = stacked.shape[1:]
    per_device = stacked.shape[0] // tensors
    device_grid = stacked.reshape((tensors, per_device) + tail_shape)
    prompt_part = device_grid[:, : pre_dev * part_rows].reshape(
        (tensors, pre_dev, part_rows) + tail_shape
    )
    prompt_part = jnp.swapaxes(prompt_part, 0, 1).reshape(
        (pre_dev, tensors * part_rows) + tail_shape
    )
    decode_part = device_grid[:, pre_dev * part_rows :].reshape((-1,) + tail_shape)
    return (prompt_part, decode_part)


def join_rows(prompt_part, decode_part, tensors):
    pre_dev = prompt_part.shape[0]
    part_rows = prompt_part.shape[1] // tensors
    tail_shape = prompt_part.shape[2:]
    leading = jnp.swapaxes(prompt_part.reshape((pre_dev, tensors, part_rows) + tail_shape), 0, 1)
    leading = leading.reshape((tensors, pre_dev * part_rows) + tail_shape)
    trailing = decode_part.reshape((tensors, -1) + tail_shape)
    return jnp.concatenate([leading, trailing], axis=1).reshape((-1,) + tail_shape)


def spread(local_rows, weights):
    return jnp.einsum(
        "rd,kdc->rkc",
        lax.all_gather(local_rows, "tensor", axis=0, tiled=True),
        weights,
        preferred_element_type=jnp.float32,
    )


def collect(operand, weights):
    return lax.psum_scatter(
        jnp.dot(operand, weights, preferred_element_type=jnp.float32).astype(jnp.bfloat16),
        "tensor",
        scatter_dimension=0,
        tiled=True,
    ).astype(jnp.float32)


def local(
    prompt_states,
    decode_states,
    cache,
    prompt_starts,
    decode_lengths,
    decode_slots,
    w_qkv,
    w_out,
    w_gate_up,
    w_down,
    gains,
):
    tensors = lax.axis_size("tensor")
    tensor_pos = lax.axis_index("tensor")
    data_pos = lax.axis_index("dp")
    pre_dev, part_rows, model_width = prompt_states.shape
    dec_part = decode_states.shape[0]
    group_len = part_rows * tensors
    dec_dev = dec_part * tensors
    ctx_part = cache.shape[2]
    head_count = model_width // HD
    prompt_own = pre_dev * part_rows
    own_rows = prompt_own + dec_part
    states = jnp.concatenate(
        [prompt_states.reshape(prompt_own, model_width), decode_states], axis=0
    )
    starts = lax.dynamic_slice_in_dim(prompt_starts, data_pos * pre_dev, pre_dev)
    slot_ids = data_pos * dec_dev + jnp.arange(dec_dev, dtype=jnp.int32)
    matches = decode_slots[None, :] == slot_ids[:, None]
    slot_length = jnp.sum(jnp.where(matches, decode_lengths[None, :], 0), axis=1)
    offsets = jnp.arange(group_len, dtype=jnp.int32)
    prompt_pos = starts[:, None] + offsets[None, :]
    own_prompt_pos = lax.dynamic_slice_in_dim(
        prompt_pos, tensor_pos * part_rows, part_rows, 1
    ).reshape(prompt_own)
    own_decode_pos = lax.dynamic_slice_in_dim(slot_length, tensor_pos * dec_part, dec_part)
    own_pos = jnp.concatenate([own_prompt_pos, own_decode_pos], axis=0)
    projected = spread(states, w_qkv)
    query_raw = projected[:, 0].astype(jnp.bfloat16)
    key_raw = projected[:, 1].astype(jnp.bfloat16)
    value_raw = projected[:, 2].astype(jnp.bfloat16)
    query_all, key_all, value_all = (
        lax.all_gather(query_raw, "tensor", axis=1, tiled=True),
        lax.all_gather(key_raw, "tensor", axis=1, tiled=True),
        lax.all_gather(value_raw, "tensor", axis=1, tiled=True),
    )
    key_own = lax.dynamic_slice_in_dim(key_all, tensor_pos * own_rows, own_rows, 0)
    value_own = lax.dynamic_slice_in_dim(value_all, tensor_pos * own_rows, own_rows, 0)
    query_prompt, query_decode = split_rows(query_all, tensors, pre_dev, part_rows)
    query_prompt = rotate(rms_scale(query_prompt.astype(jnp.float32), gains[0]), prompt_pos).astype(
        jnp.bfloat16
    )
    query_decode = rotate(
        rms_scale(query_decode.astype(jnp.float32), gains[0]), slot_length
    ).astype(jnp.bfloat16)
    key_new = rotate(rms_scale(key_own.astype(jnp.float32), gains[1]), own_pos).astype(jnp.bfloat16)
    scale_factor = HD ** (-0.5)
    cache_pos = tensor_pos * ctx_part + jnp.arange(ctx_part, dtype=jnp.int32)
    prompt_q = query_prompt.reshape(pre_dev, group_len, head_count, HD)
    prompt_keys = cache[0, :pre_dev].reshape(pre_dev, ctx_part, head_count, HD)
    prompt_values = cache[1, :pre_dev].reshape(pre_dev, ctx_part, head_count, HD)
    fresh_keys = key_new[:prompt_own].reshape(pre_dev, part_rows, head_count, HD)
    fresh_values = value_own[:prompt_own].reshape(pre_dev, part_rows, head_count, HD)
    cached_scores = jnp.einsum(
        "aihe,ajhe->ahij", prompt_q, prompt_keys, preferred_element_type=jnp.float32
    )
    fresh_scores = jnp.einsum(
        "aihe,ajhe->ahij", prompt_q, fresh_keys, preferred_element_type=jnp.float32
    )
    prompt_scores = jnp.concatenate([cached_scores, fresh_scores], axis=-1) * scale_factor
    key_offsets = tensor_pos * part_rows + jnp.arange(part_rows, dtype=jnp.int32)
    live_cached = jnp.broadcast_to(
        (cache_pos[None, :] < starts[:, None])[:, None, None, :], (pre_dev, 1, group_len, ctx_part)
    )
    live_fresh = jnp.broadcast_to(
        (key_offsets[None, :] <= offsets[:, None])[None, None], (pre_dev, 1, group_len, part_rows)
    )
    prompt_live = jnp.concatenate([live_cached, live_fresh], axis=-1)
    prompt_masked = jnp.where(prompt_live, prompt_scores, MASKED_SCORE)
    prompt_top = jnp.max(prompt_masked, axis=-1)
    decode_q = query_decode.reshape(dec_dev, head_count, HD)
    decode_keys = cache[0, pre_dev:].reshape(dec_dev, ctx_part, head_count, HD)
    decode_values = cache[1, pre_dev:].reshape(dec_dev, ctx_part, head_count, HD)
    own_keys = key_new[prompt_own:].reshape(dec_part, head_count, HD)
    own_values = value_own[prompt_own:].reshape(dec_part, head_count, HD)
    decode_cached = jnp.einsum(
        "she,sjhe->shj", decode_q, decode_keys, preferred_element_type=jnp.float32
    )
    decode_fresh = jnp.einsum(
        "she,jhe->shj", decode_q, own_keys, preferred_element_type=jnp.float32
    )
    decode_scores = jnp.concatenate([decode_cached, decode_fresh], axis=-1) * scale_factor
    live_slots = (cache_pos[None, :] < slot_length[:, None])[:, None, :]
    own_ids = tensor_pos * dec_part + jnp.arange(dec_part, dtype=jnp.int32)
    live_owned = (jnp.arange(dec_dev, dtype=jnp.int32)[:, None] == own_ids[None, :])[:, None, :]
    decode_live = jnp.concatenate([live_slots, live_owned], axis=-1)
    decode_masked = jnp.where(decode_live, decode_scores, MASKED_SCORE)
    decode_top = jnp.max(decode_masked, axis=-1)
    prompt_weights = jnp.where(prompt_live, jnp.exp(prompt_masked - prompt_top[..., None]), 0.0)
    prompt_total = jnp.sum(prompt_weights, axis=-1)
    prompt_probs = prompt_weights.astype(jnp.bfloat16)
    prompt_mixed = jnp.einsum(
        "ahij,ajhe->aihe",
        prompt_probs[..., :ctx_part],
        prompt_values,
        preferred_element_type=jnp.float32,
    )
    prompt_mixed = prompt_mixed + jnp.einsum(
        "ahij,ajhe->aihe",
        prompt_probs[..., ctx_part:],
        fresh_values,
        preferred_element_type=jnp.float32,
    )
    decode_weights = jnp.where(decode_live, jnp.exp(decode_masked - decode_top[..., None]), 0.0)
    decode_total = jnp.sum(decode_weights, axis=-1)
    decode_probs = decode_weights.astype(jnp.bfloat16)
    decode_mixed = jnp.einsum(
        "shj,sjhe->she",
        decode_probs[..., :ctx_part],
        decode_values,
        preferred_element_type=jnp.float32,
    )
    decode_mixed = decode_mixed + jnp.einsum(
        "shj,jhe->she", decode_probs[..., ctx_part:], own_values, preferred_element_type=jnp.float32
    )
    totals = join_rows(jnp.swapaxes(prompt_total, 1, 2), decode_total, tensors)
    mixed = join_rows(
        prompt_mixed.reshape(pre_dev, group_len, model_width),
        decode_mixed.reshape(dec_dev, model_width),
        tensors,
    )
    tops = join_rows(jnp.swapaxes(prompt_top, 1, 2), decode_top, tensors)
    got_tops, got_totals, got_mixed = (
        lax.all_to_all(tops, "tensor", split_axis=0, concat_axis=0, tiled=True),
        lax.all_to_all(totals, "tensor", split_axis=0, concat_axis=0, tiled=True),
        lax.all_to_all(mixed, "tensor", split_axis=0, concat_axis=0, tiled=True),
    )
    got_tops = got_tops.reshape(tensors, own_rows, head_count)
    got_totals = got_totals.reshape(tensors, own_rows, head_count)
    got_mixed = got_mixed.reshape(tensors, own_rows, head_count, HD)
    highest = jnp.max(got_tops, axis=0)
    factors = jnp.exp(got_tops - highest[None])
    total_all = jnp.sum(got_totals * factors, axis=0)
    shares = lax.optimization_barrier((got_mixed * factors[..., None]).astype(jnp.bfloat16))
    mixed_all = jnp.sum(shares.astype(jnp.float32), axis=0)
    attended_own = (
        (mixed_all / total_all[..., None]).reshape(own_rows, model_width).astype(jnp.bfloat16)
    )
    my_columns = lax.all_to_all(attended_own, "tensor", split_axis=1, concat_axis=0, tiled=True)
    attn_sum = collect(my_columns, w_out)
    hidden = (states.astype(jnp.float32) + rms_scale(attn_sum, gains[2])).astype(jnp.bfloat16)
    gate_up = spread(hidden, w_gate_up)
    activated = (jax.nn.silu(gate_up[:, 0]) * gate_up[:, 1]).astype(jnp.bfloat16)
    ffn_sum = collect(activated, w_down)
    output = (hidden.astype(jnp.float32) + rms_scale(ffn_sum, gains[3])).astype(jnp.bfloat16)
    prompt_out = output[:prompt_own].reshape(pre_dev, part_rows, model_width)
    everyone = lax.all_gather(output[prompt_own:], ("dp", "tensor"), axis=0, tiled=True)
    wanted = lax.dynamic_slice_in_dim(
        decode_slots, (data_pos * tensors + tensor_pos) * dec_part, dec_part
    )
    decode_out = jnp.take(everyone, wanted, axis=0)
    new_prompt_kv = jnp.stack([key_new[:prompt_own], value_own[:prompt_own]]).reshape(
        2, pre_dev, part_rows, model_width
    )
    new_decode_kv = jnp.stack([key_new[prompt_own:], value_own[prompt_own:]])
    return (prompt_out, decode_out, new_prompt_kv, new_decode_kv)


Z = 4
BLOCK_PAD = 16


def z_pairs(targets):
    return [(z * 2 + c, t * 2 + c) for z in range(Z) for t in targets(z) for c in range(2)]


CORE = [(i, i ^ 1) for i in range(2 * Z)]
UP = [z_pairs(lambda z, k=k: [z + 1] if k <= z < Z - 1 else []) for k in range(Z - 1)]
DOWN = [z_pairs(lambda z, k=k: [z - 1] if 0 < z <= Z - 1 - k else []) for k in range(Z - 1)]
TURN = [z_pairs(lambda z, k=k: [(z + k) % Z]) for k in range(1, Z)]
ENDS = z_pairs(lambda z: {0: [1], 3: [2]}.get(z, []))
RISE = [z_pairs(lambda z: [z + 1] if z < 2 else []), z_pairs(lambda z: [z + 1] if z < 3 else [])]
FALL = [z_pairs(lambda z: [z - 1] if z > 1 else []), z_pairs(lambda z: [z - 1] if z > 0 else [])]


def send(values, pairs):
    return lax.ppermute(values, "tensor", pairs)


def line_gather(values, chip):
    rising = falling = values
    rises, falls = [], []
    for step in range(Z - 1):
        rising = send(rising, UP[step])
        falling = send(falling, DOWN[step])
        rises.append(rising)
        falls.append(falling)
    return [values] + [
        jnp.where(chip >= k, rises[k - 1], falls[Z - 1 - k]) for k in range(1, Z)
    ]


def small_gather(values, chip, core):
    pair = jnp.stack([values, send(values, CORE)])
    pair = jnp.where(core == 0, pair, pair[::-1])
    chips = jnp.stack([pair] + [send(pair, TURN[k]) for k in range(Z - 1)])
    order = (chip - jnp.arange(Z, dtype=jnp.int32)) % Z
    return jnp.take(chips, order, axis=0).reshape((2 * Z,) + values.shape)


def small_sum(values):
    total = values + send(values, CORE)
    parts = [send(total, TURN[k]) for k in range(Z - 1)]
    return total + parts[1] + (parts[0] + parts[2])


def exchange(blocks, chip, core):
    mine = lax.dynamic_index_in_dim(blocks, core, 1, keepdims=False)
    other = lax.dynamic_index_in_dim(blocks, 1 - core, 1, keepdims=False)
    both = jnp.stack([mine, send(other, CORE)], axis=1)
    got = [lax.dynamic_index_in_dim(both, chip, 0, keepdims=False)]
    for k in range(1, Z):
        part = lax.dynamic_index_in_dim(both, (chip + k) % Z, 0, keepdims=False)
        got.append(send(part, TURN[k - 1]))
    return got


def data_gather(values, data_pos):
    first = jnp.stack([values, lax.ppermute(values, "dp", [(i, i ^ 1) for i in range(4)])])
    second = lax.ppermute(first, "dp", [(i, i ^ 2) for i in range(4)])
    both = jnp.concatenate([first, second])
    return jnp.take(both, jnp.arange(4, dtype=jnp.int32) ^ data_pos, axis=0)


def params(limit=56):
    return pltpu.CompilerParams(vmem_limit_bytes=limit * 2**20)


def project_kernel(where, xa, xb, w, pb_in, db_in, xs_in, prompt_out, decode_out, rows_out):
    step = pl.program_id(0)

    def work(x):
        rows = x[...]
        rows_out[0] = rows
        for part in range(3):
            made = jnp.dot(rows, w[part], preferred_element_type=jnp.float32)
            made = made.astype(jnp.bfloat16)
            cols = pl.ds(part * 256, 256)
            prompt_out[0, 0, :, cols] = made[:64]
            prompt_out[1, 0, :, cols] = made[64:128]
            decode_out[0, :, cols] = made[128:]

    @pl.when(step == 0)
    def _():
        work(xa)

    @pl.when(step == 1)
    def _():
        work(xb)


def project(where, xa, xb, w, buffers):
    rows = xa.shape[0]
    width = xa.shape[1]
    grid_spec = pltpu.PrefetchScalarGridSpec(
        num_scalar_prefetch=1,
        grid=(2,),
        in_specs=[
            pl.BlockSpec((rows, width), lambda i, s: (0, 0)),
            pl.BlockSpec((rows, width), lambda i, s: (0, 0)),
            pl.BlockSpec(w.shape, lambda i, s: (0, 0, 0)),
            pl.BlockSpec(memory_space=pl.ANY),
            pl.BlockSpec(memory_space=pl.ANY),
            pl.BlockSpec(memory_space=pl.ANY),
        ],
        out_specs=[
            pl.BlockSpec((2, 1, 64, 768), lambda i, s: (0, s[i], 0, 0)),
            pl.BlockSpec((1, rows - 128, 768), lambda i, s: (s[i], 0, 0)),
            pl.BlockSpec((1, rows, width), lambda i, s: (s[i], 0, 0)),
        ],
    )
    return pl.pallas_call(
        project_kernel,
        grid_spec=grid_spec,
        out_shape=[jax.ShapeDtypeStruct(b.shape, b.dtype) for b in buffers],
        input_output_aliases={4: 0, 5: 1, 6: 2},
        compiler_params=params(),
        cost_estimate=pl.CostEstimate(
            flops=4 * rows * width * 768, bytes_accessed=9 * 2**20, transcendentals=0
        ),
        name="project",
    )(where, xa, xb, w, *buffers)


def swap_pairs(values):
    lane = lax.broadcasted_iota(jnp.int32, values.shape, 1)
    after = pltpu.roll(values, HD - 1, 1)
    before = pltpu.roll(values, 1, 1)
    return jnp.where(lane % 2 == 0, after, before)


def attend_kernel(starts, q, k, v, ck, cv, scales, gain, cosine, sine, cached_at, out, key_out):
    prompt = pl.program_id(0)
    scale = scales[0]
    cos_t, sin_t = cosine[0], sine[0]

    def turn(raw, which):
        val = raw[0].astype(jnp.float32) * scale[:, which : which + 1] * gain[which : which + 1, :]
        return (val * cos_t + swap_pairs(val) * sin_t).astype(jnp.bfloat16)

    queries = turn(q, 0)
    keys = turn(k, 1)
    key_out[0] = keys
    dims = (((1,), (1,)), ((), ()))
    factor = HD ** (-0.5)
    rows = queries.shape[0]
    old = lax.dot_general(queries, ck[0], dims, preferred_element_type=jnp.float32) * factor
    new = lax.dot_general(queries, keys, dims, preferred_element_type=jnp.float32) * factor
    live_old = cached_at[...] < starts[prompt]
    live_new = lax.broadcasted_iota(jnp.int32, (rows, rows), 1) <= lax.broadcasted_iota(
        jnp.int32, (rows, rows), 0
    )
    old = jnp.where(live_old, old, MASKED_SCORE)
    new = jnp.where(live_new, new, MASKED_SCORE)
    top = jnp.maximum(
        jnp.max(old, axis=1, keepdims=True), jnp.max(new, axis=1, keepdims=True)
    )
    old = jnp.exp(old - top)
    new = jnp.exp(new - top)
    total = jnp.sum(old, axis=1, keepdims=True) + jnp.sum(new, axis=1, keepdims=True)
    mixed = jnp.dot(old.astype(jnp.bfloat16), cv[0], preferred_element_type=jnp.float32)
    mixed = mixed + jnp.dot(new.astype(jnp.bfloat16), v[0], preferred_element_type=jnp.float32)
    out[0] = (mixed / total).astype(jnp.bfloat16)


def attend(starts, qkv, ck, cv, scales, gain, cosine, sine, cached_at):
    group = qkv.shape[1]
    ctx = ck.shape[1]
    head = lambda off: pl.BlockSpec((1, group, HD), lambda p, h, s: (p, 0, off + h))
    grid_spec = pltpu.PrefetchScalarGridSpec(
        num_scalar_prefetch=1,
        grid=(2, 2),
        in_specs=[
            head(0),
            head(2),
            head(4),
            pl.BlockSpec((1, ctx, HD), lambda p, h, s: (p, 0, h)),
            pl.BlockSpec((1, ctx, HD), lambda p, h, s: (p, 0, h)),
            pl.BlockSpec((1, group, 2), lambda p, h, s: (p, 0, 0)),
            pl.BlockSpec((2, HD), lambda p, h, s: (0, h)),
            pl.BlockSpec((1, group, HD), lambda p, h, s: (p, 0, 0)),
            pl.BlockSpec((1, group, HD), lambda p, h, s: (p, 0, 0)),
            pl.BlockSpec((1, ctx), lambda p, h, s: (0, 0)),
        ],
        out_specs=[head(0), head(0)],
    )
    made = jax.ShapeDtypeStruct((2, group, 2 * HD), jnp.bfloat16)
    return pl.pallas_call(
        attend_kernel,
        grid_spec=grid_spec,
        out_shape=[made, made],
        compiler_params=params(),
        cost_estimate=pl.CostEstimate(
            flops=16 * group * (group + ctx) * HD,
            bytes_accessed=6 * 2**20,
            transcendentals=4 * group * (group + ctx),
        ),
        name="attend",
    )(starts, qkv, qkv, qkv, ck, cv, scales, gain, cosine, sine, cached_at)


def mix_kernel(where, *refs):
    att = refs[:8]
    wparts = refs[8:16]
    dec, xs, dec_x, gain, out, lhs, w, sems = refs[16:]
    step = pl.program_id(0)
    data = where[8]

    def copies():
        made = []
        for i in range(8):
            cols = pl.ds(pl.multiple_of(where[i] * 256, 256), 256)
            made.append(pltpu.make_async_copy(att[i], lhs.at[:, :, :, cols], sems.at[i]))
        number = 8
        for core in range(2):
            for half in range(2):
                for hop in range(2):
                    part = wparts[core * 4 + half * 2 + hop]
                    for lead in range(2):
                        if half == 0:
                            rel = lead + 2 * hop
                        else:
                            rel = 2 * lead + hop
                        row = pl.multiple_of((data ^ rel) * 64, 64)
                        for k in range(4):
                            block = where[2 * k + core]
                            made.append(
                                pltpu.make_async_copy(
                                    part.at[lead, k],
                                    w.at[block, pl.ds(row, 64), pl.ds(half * 1024, 1024)],
                                    sems.at[number],
                                )
                            )
                            number += 1
        return made

    @pl.when(step == 0)
    def _():
        made = copies()
        for copy in made:
            copy.start()
        for copy in made:
            copy.wait()

    pieces = []
    for c in range(2):
        pieces += [lhs[0, step * 2 + c], lhs[1, step * 2 + c], dec[c]]
    rows = jnp.concatenate(pieces, axis=0)
    total = jnp.zeros((rows.shape[0], w.shape[2]), jnp.float32)
    for t in range(8):
        total = total + jnp.dot(
            rows[:, t * 256 : (t + 1) * 256], w[t], preferred_element_type=jnp.float32
        )
    inv = lax.rsqrt(jnp.mean(total * total, axis=1, keepdims=True) + EPSILON)
    total = total * inv * gain[2:3, :]
    per = 128 + BLOCK_PAD
    for c in range(2):
        base = c * per
        out[c, :128] = (
            xs[c, :128].astype(jnp.float32) + total[base : base + 128]
        ).astype(jnp.bfloat16)
        out[c, 128:] = (
            dec_x[c].astype(jnp.float32) + total[base + 128 : base + per]
        ).astype(jnp.bfloat16)


def mix(where, att, wparts, dec, xs, dec_x, gains):
    width = xs.shape[2]
    any_spec = pl.BlockSpec(memory_space=pl.ANY)
    grid_spec = pltpu.PrefetchScalarGridSpec(
        num_scalar_prefetch=1,
        grid=(Z,),
        in_specs=[any_spec] * 16
        + [
            pl.BlockSpec((2, BLOCK_PAD, width), lambda i, s: (i, 0, 0)),
            pl.BlockSpec((2, xs.shape[1], width), lambda i, s: (i, 0, 0)),
            pl.BlockSpec((2, BLOCK_PAD, width), lambda i, s: (i, 0, 0)),
            pl.BlockSpec(gains.shape, lambda i, s: (0, 0)),
        ],
        out_specs=pl.BlockSpec((2, 128 + BLOCK_PAD, width), lambda i, s: (i, 0, 0)),
        scratch_shapes=[
            pltpu.VMEM((2, 8, 64, width), jnp.bfloat16),
            pltpu.VMEM((8, 256, width), jnp.bfloat16),
            pltpu.SemaphoreType.DMA((8 + 64,)),
        ],
    )
    return pl.pallas_call(
        mix_kernel,
        grid_spec=grid_spec,
        out_shape=jax.ShapeDtypeStruct((8, 128 + BLOCK_PAD, width), jnp.bfloat16),
        compiler_params=params(),
        cost_estimate=pl.CostEstimate(
            flops=2 * 8 * 144 * width * width, bytes_accessed=22 * 2**20, transcendentals=0
        ),
        name="mix",
    )(where, *att, *wparts, dec, xs, dec_x, gains)


def forward_kernel(where, hidden, wgu, wd, mine, other, acc):
    step = pl.program_id(0)
    per = hidden.shape[1]
    rows = hidden[...].reshape(2 * per, hidden.shape[2])
    gate = jnp.dot(rows, wgu[0], preferred_element_type=jnp.float32)
    up = jnp.dot(rows, wgu[1], preferred_element_type=jnp.float32)
    act = (gate / (1.0 + jnp.exp(-gate)) * up).astype(jnp.bfloat16)
    part = jnp.dot(act, wd[...], preferred_element_type=jnp.float32).reshape(acc.shape)

    @pl.when(step == 0)
    def _():
        acc[...] = part

    @pl.when(step > 0)
    def _():
        acc[...] += part

    @pl.when(step == pl.num_programs(0) - 1)
    def _():
        core = where[1]
        mine[...] = acc[core, : mine.shape[0]].astype(jnp.bfloat16)
        other[...] = acc[1 - core, : mine.shape[0]].astype(jnp.bfloat16)


def forward(where, hidden, wgu, wd, rows):
    per, width = hidden.shape[1:]
    units = wd.shape[0]
    tile = 256
    grid_spec = pltpu.PrefetchScalarGridSpec(
        num_scalar_prefetch=1,
        grid=(units // tile,),
        in_specs=[
            pl.BlockSpec((2, per, width), lambda i, s: (s[0], 0, 0)),
            pl.BlockSpec((2, width, tile), lambda i, s: (0, 0, i)),
            pl.BlockSpec((tile, width), lambda i, s: (i, 0)),
        ],
        out_specs=[pl.BlockSpec((rows, width), lambda i, s: (0, 0))] * 2,
        scratch_shapes=[pltpu.VMEM((2, per, width), jnp.float32)],
    )
    made = jax.ShapeDtypeStruct((rows, width), jnp.bfloat16)
    return pl.pallas_call(
        forward_kernel,
        grid_spec=grid_spec,
        out_shape=[made, made],
        compiler_params=params(),
        cost_estimate=pl.CostEstimate(
            flops=12 * per * width * units, bytes_accessed=14 * 2**20, transcendentals=0
        ),
        name="forward",
    )(where, hidden, wgu, wd)


def tables(positions):
    lanes = jnp.arange(HD, dtype=jnp.int32)
    freq_index = (lanes // 2).astype(jnp.float32)
    inv_freq = jnp.power(ROPE_BASE, -2.0 * freq_index / HD)
    angles = positions.astype(jnp.float32)[..., None] * inv_freq
    sign = jnp.where(lanes % 2 == 0, -1.0, 1.0)
    return jnp.cos(angles), jnp.sin(angles) * sign


def narrow_sum(*terms):
    total = terms[0].astype(jnp.float32)
    for term in terms[1:]:
        total = total + term.astype(jnp.float32)
    return total.astype(jnp.bfloat16)


def after(values, *others):
    return lax.optimization_barrier((values,) + others)[0]


def local_heads(
    prompt_states,
    decode_states,
    cache,
    prompt_starts,
    decode_lengths,
    decode_slots,
    w_qkv,
    w_out,
    w_gate_up,
    w_down,
    gains,
):
    place = lax.axis_index("tensor")
    chip, core = place // 2, place % 2
    data_pos = lax.axis_index("dp")
    pre_dev, part_rows, width = prompt_states.shape
    dec_part = decode_states.shape[0]
    group = part_rows * 8
    dec_dev = dec_part * 8
    ctx_part = cache.shape[2]
    heads = width // HD
    own_rows = pre_dev * part_rows + dec_part
    states = jnp.concatenate(
        [prompt_states.reshape(pre_dev * part_rows, width), decode_states], axis=0
    )
    starts = lax.dynamic_slice_in_dim(prompt_starts, data_pos * pre_dev, pre_dev)
    slot_ids = data_pos * dec_dev + jnp.arange(dec_dev, dtype=jnp.int32)
    matches = decode_slots[None, :] == slot_ids[:, None]
    slot_length = jnp.sum(jnp.where(matches, decode_lengths[None, :], 0), axis=1)
    prompt_pos = starts[:, None] + jnp.arange(group, dtype=jnp.int32)[None, :]
    cos_p, sin_p = tables(prompt_pos)
    cos_d, sin_d = tables(slot_length)
    my_gains = lax.dynamic_slice_in_dim(gains[:2], place * 256, 256, 1)

    chips_at = (chip - jnp.arange(Z, dtype=jnp.int32)) % Z
    blocks_at = jnp.stack([chips_at * 2 + core, chips_at * 2 + 1 - core], axis=1).astype(jnp.int32)
    lines = line_gather(states, chip)
    buffers = (
        jnp.zeros((2, 8, 64, 768), jnp.bfloat16),
        jnp.zeros((8, dec_part, 768), jnp.bfloat16),
        jnp.zeros((8, own_rows, width), jnp.bfloat16),
    )
    for k in range(Z):
        buffers = project(blocks_at[k], lines[k], send(lines[k], CORE), w_qkv, buffers)
    prompt_raw, decode_raw, xs = buffers
    prompt_raw = prompt_raw.reshape(pre_dev, group, 768)
    decode_raw = decode_raw.reshape(dec_dev, 768)

    prompt_cache = cache[:, :pre_dev].reshape(2, pre_dev, ctx_part, Z, 2, 256)
    prompt_cache = jnp.transpose(prompt_cache, (3, 4, 0, 1, 2, 5))
    prompt_cache = after(prompt_cache, lines[2])
    got = exchange(prompt_cache, chip, core)
    got = jnp.stack(got).reshape(8, 2, pre_dev, ctx_part, 256)
    got = jnp.transpose(got, (1, 2, 0, 3, 4)).reshape(2, pre_dev, 8 * ctx_part, 256)
    cached_at = (
        blocks_at.reshape(8, 1) * ctx_part + jnp.arange(ctx_part, dtype=jnp.int32)[None, :]
    ).reshape(1, 8 * ctx_part)

    share = w_out.shape[0] // 4
    w_share = lax.dynamic_slice_in_dim(w_out, data_pos * share, share)
    w_share = after(w_share, lines[3])
    w_line = jnp.stack(line_gather(w_share, chip))
    half = width // 2
    first, second = w_line[:, :, :half], w_line[:, :, half:]
    along_x = lambda v: lax.ppermute(v, "dp", [(i, i ^ 1) for i in range(4)])
    along_y = lambda v: lax.ppermute(v, "dp", [(i, i ^ 2) for i in range(4)])
    first_pair = jnp.stack([first, along_x(first)])
    second_pair = jnp.stack([second, along_y(second)])
    w_own = [first_pair, along_y(first_pair), second_pair, along_x(second_pair)]
    w_parts = w_own + [send(part, CORE) for part in w_own]

    both = jnp.concatenate([prompt_raw.reshape(-1, 768), decode_raw])[:, :512].astype(jnp.float32)
    squares = jnp.sum((both * both).reshape(-1, 2, 256), axis=-1)
    squares = small_sum(jnp.swapaxes(squares, 0, 1))
    scales = jnp.swapaxes(lax.rsqrt(squares / width + EPSILON), 0, 1)
    prompt_rows = pre_dev * group
    attended, key_new = attend(
        starts,
        prompt_raw,
        got[0],
        got[1],
        scales[:prompt_rows].reshape(pre_dev, group, 2),
        my_gains,
        cos_p,
        sin_p,
        cached_at,
    )

    def turn(raw, scale, gain):
        val = raw.astype(jnp.float32) * scale * gain
        val = val.reshape(raw.shape[0], -1, HD)
        pairs = val.reshape(val.shape[:-1] + (HD // 2, 2))
        swapped = pairs[..., ::-1].reshape(val.shape)
        return (val * cos_d[:, None] + swapped * sin_d[:, None]).astype(jnp.bfloat16)

    dec_scales = scales[prompt_rows:]
    query_mine = turn(decode_raw[:, :256], dec_scales[:, :1], my_gains[0])
    key_mine = turn(decode_raw[:, 256:512], dec_scales[:, 1:], my_gains[1])
    value_mine = decode_raw[:, 512:].reshape(dec_dev, 2, HD)
    query_all = small_gather(query_mine.reshape(dec_dev, 256), chip, core)
    query_all = jnp.swapaxes(query_all, 0, 1).reshape(dec_dev, heads, HD)
    scale_factor = HD ** (-0.5)
    decode_keys = cache[0, pre_dev:].reshape(dec_dev, ctx_part, heads, HD)
    decode_values = cache[1, pre_dev:].reshape(dec_dev, ctx_part, heads, HD)
    cache_pos = place * ctx_part + jnp.arange(ctx_part, dtype=jnp.int32)
    live = (cache_pos[None, :] < slot_length[:, None])[:, None, :]
    scores = jnp.einsum(
        "she,sjhe->shj", query_all, decode_keys, preferred_element_type=jnp.float32
    )
    scores = jnp.where(live, scores * scale_factor, MASKED_SCORE)
    tops = jnp.max(scores, axis=-1)
    weights = jnp.where(live, jnp.exp(scores - tops[..., None]), 0.0)
    sums = jnp.sum(weights, axis=-1)
    mixed = jnp.einsum(
        "shj,sjhe->she",
        weights.astype(jnp.bfloat16),
        decode_values,
        preferred_element_type=jnp.float32,
    )
    parts = jnp.concatenate(
        [
            jnp.transpose(mixed.reshape(dec_dev, 8, 256), (1, 0, 2)),
            jnp.transpose(tops.reshape(dec_dev, 8, 2), (1, 0, 2)),
            jnp.transpose(sums.reshape(dec_dev, 8, 2), (1, 0, 2)),
        ],
        axis=-1,
    )
    arrived = exchange(parts.reshape(Z, 2, dec_dev, 260), chip, core)
    arrived = jnp.stack(arrived).reshape(8, dec_dev, 260)
    got_mixed = arrived[..., :256].reshape(8, dec_dev, 2, HD)
    got_tops, got_sums = arrived[..., 256:258], arrived[..., 258:]
    own_score = (
        jnp.sum(query_mine.astype(jnp.float32) * key_mine.astype(jnp.float32), axis=-1)
        * scale_factor
    )
    highest = jnp.maximum(jnp.max(got_tops, axis=0), own_score)
    factors = jnp.exp(got_tops - highest[None])
    own_weight = jnp.exp(own_score - highest)
    total = jnp.sum(got_sums * factors, axis=0) + own_weight
    summed = jnp.sum(got_mixed * factors[..., None], axis=0)
    summed = summed + own_weight.astype(jnp.bfloat16).astype(jnp.float32)[
        ..., None
    ] * value_mine.astype(jnp.float32)
    dec_attended = (summed / total[..., None]).reshape(dec_dev, 256).astype(jnp.bfloat16)
    wanted = lax.dynamic_slice_in_dim(decode_slots, data_pos * dec_dev, dec_dev)
    by_request = jnp.take(
        data_gather(dec_attended, data_pos).reshape(4 * dec_dev, 256), wanted, axis=0
    )
    pad = lambda v: jnp.pad(
        v.reshape(8, dec_part, width), ((0, 0), (0, BLOCK_PAD - dec_part), (0, 0))
    )
    dec_rows = small_gather(by_request, chip, core)
    dec_rows = pad(jnp.swapaxes(dec_rows, 0, 1).reshape(dec_dev, width))
    dec_x = data_gather(xs[:, own_rows - dec_part :].reshape(dec_dev, width), data_pos)
    dec_x = pad(jnp.take(dec_x.reshape(4 * dec_dev, width), wanted, axis=0))

    att_lines = line_gather(attended.reshape(pre_dev, 8, part_rows, 256), chip)
    att = []
    for line in att_lines:
        att += [line, send(line, CORE)]
    where = jnp.concatenate([blocks_at.reshape(8), data_pos[None].astype(jnp.int32)])
    hidden = mix(where, att, w_parts, dec_rows, xs, dec_x, gains)

    orders = jnp.array([[3, 2, 1, 0], [3, 2, 0, 1], [0, 1, 3, 2], [0, 1, 2, 3]], jnp.int32)
    order = lax.dynamic_index_in_dim(orders, chip, 0, keepdims=False)
    sums = []
    for k in range(Z):
        at = jnp.stack([order[k], core]).astype(jnp.int32)
        mine, other = forward(at, hidden, w_gate_up, w_down, own_rows)
        sums.append(narrow_sum(mine, send(other, CORE)))
    came = send(sums[0], ENDS)
    is_end = (chip == 0) | (chip == 3)
    load = narrow_sum(jnp.where(is_end, sums[1], sums[0]), came)
    up, down = send(load, RISE[0]), send(load, FALL[0])
    up = send(narrow_sum(jnp.where(chip == 1, sums[1], sums[2]), up), RISE[1])
    down = send(narrow_sum(jnp.where(chip == 2, sums[1], sums[2]), down), FALL[1])
    ffn_sum = sums[3].astype(jnp.float32) + up.astype(jnp.float32) + down.astype(jnp.float32)
    hidden_own = lax.dynamic_index_in_dim(hidden, place, 0, keepdims=False)[:own_rows]
    output = (hidden_own.astype(jnp.float32) + rms_scale(ffn_sum, gains[3])).astype(jnp.bfloat16)
    prompt_out = output[: own_rows - dec_part].reshape(pre_dev, part_rows, width)
    decode_out = output[own_rows - dec_part :]

    fresh = jnp.stack([key_new, prompt_raw[:, :, 512:]])
    fresh = fresh.reshape(2, pre_dev, 8, part_rows, 256)
    fresh = jnp.transpose(fresh, (2, 0, 1, 3, 4)).reshape(8, 2, pre_dev * part_rows, 256)
    fresh_dec = jnp.stack([key_mine.reshape(dec_dev, 256), decode_raw[:, 512:]])
    fresh_dec = jnp.transpose(fresh_dec.reshape(2, 8, dec_part, 256), (1, 0, 2, 3))
    fresh = jnp.concatenate([fresh, fresh_dec], axis=2)
    fresh = after(fresh, hidden)
    came = exchange(fresh.reshape(Z, 2, 2, own_rows, 256), chip, core)
    came = jnp.take(jnp.stack(came), chips_at, axis=0)
    came = jnp.where(core == 0, came, came[:, ::-1]).reshape(8, 2, own_rows, 256)
    came = jnp.transpose(came, (1, 2, 0, 3)).reshape(2, own_rows, width)
    new_prompt_kv = came[:, : own_rows - dec_part].reshape(2, pre_dev, part_rows, width)
    new_decode_kv = came[:, own_rows - dec_part :]
    return (prompt_out, decode_out, new_prompt_kv, new_decode_kv)


def fits_heads(mesh):
    return mesh.shape["tensor"] == 2 * Z and mesh.shape["dp"] == 4


def solution(mesh):
    in_specs = (
        P("dp", "tensor", None),
        P(("dp", "tensor"), None),
        P(None, "dp", "tensor", None),
        P(),
        P(),
        P(),
        P(None, None, "tensor"),
        P("tensor", None),
        P(None, None, "tensor"),
        P("tensor", None),
        P(),
    )
    out_specs = (
        P("dp", "tensor", None),
        P(("dp", "tensor"), None),
        P(None, "dp", "tensor", None),
        P(None, ("dp", "tensor"), None),
    )
    body = local_heads if fits_heads(mesh) else local
    return jax.shard_map(body, mesh=mesh, in_specs=in_specs, out_specs=out_specs, check_vma=False)
```

```python
import functools

import jax
import jax.numpy as jnp
from jax import lax
from jax.experimental import pallas as pl
from jax.experimental.pallas import tpu as pltpu
from jax.sharding import PartitionSpec as P

HD = 128


EPSILON = 1e-06
ROPE_BASE = 500000.0
MASKED_SCORE = -1e30


def rms_scale(values, gain_vec):
    return (
        values * lax.rsqrt(jnp.mean(values * values, axis=-1, keepdims=True) + EPSILON) * gain_vec
    )


def rotate(values, positions):
    full_shape = values.shape
    paired = values.reshape(full_shape[:-1] + (full_shape[-1] // HD, HD // 2, 2))
    freq_index = jnp.arange(HD // 2, dtype=jnp.float32)
    inv_freq = jnp.power(ROPE_BASE, -2.0 * freq_index / HD)
    angles = positions.astype(jnp.float32)[..., None, None] * inv_freq
    cosine = jnp.cos(angles)
    sine_values = jnp.sin(angles)
    even_part = paired[..., 0]
    odd_part = paired[..., 1]
    turned = jnp.stack(
        [even_part * cosine - odd_part * sine_values, even_part * sine_values + odd_part * cosine],
        axis=-1,
    )
    return turned.reshape(full_shape)


def split_rows(stacked, tensors, pre_dev, part_rows):
    tail_shape = stacked.shape[1:]
    per_device = stacked.shape[0] // tensors
    device_grid = stacked.reshape((tensors, per_device) + tail_shape)
    prompt_part = device_grid[:, : pre_dev * part_rows].reshape(
        (tensors, pre_dev, part_rows) + tail_shape
    )
    prompt_part = jnp.swapaxes(prompt_part, 0, 1).reshape(
        (pre_dev, tensors * part_rows) + tail_shape
    )
    decode_part = device_grid[:, pre_dev * part_rows :].reshape((-1,) + tail_shape)
    return (prompt_part, decode_part)


def join_rows(prompt_part, decode_part, tensors):
    pre_dev = prompt_part.shape[0]
    part_rows = prompt_part.shape[1] // tensors
    tail_shape = prompt_part.shape[2:]
    leading = jnp.swapaxes(prompt_part.reshape((pre_dev, tensors, part_rows) + tail_shape), 0, 1)
    leading = leading.reshape((tensors, pre_dev * part_rows) + tail_shape)
    trailing = decode_part.reshape((tensors, -1) + tail_shape)
    return jnp.concatenate([leading, trailing], axis=1).reshape((-1,) + tail_shape)


def spread(local_rows, weights):
    return jnp.einsum(
        "rd,kdc->rkc",
        lax.all_gather(local_rows, "tensor", axis=0, tiled=True),
        weights,
        preferred_element_type=jnp.float32,
    )


def collect(operand, weights):
    return lax.psum_scatter(
        jnp.dot(operand, weights, preferred_element_type=jnp.float32).astype(jnp.bfloat16),
        "tensor",
        scatter_dimension=0,
        tiled=True,
    ).astype(jnp.float32)


def local(
    prompt_states,
    decode_states,
    cache,
    prompt_starts,
    decode_lengths,
    decode_slots,
    w_qkv,
    w_out,
    w_gate_up,
    w_down,
    gains,
):
    tensors = lax.axis_size("tensor")
    tensor_pos = lax.axis_index("tensor")
    data_pos = lax.axis_index("dp")
    pre_dev, part_rows, model_width = prompt_states.shape
    dec_part = decode_states.shape[0]
    group_len = part_rows * tensors
    dec_dev = dec_part * tensors
    ctx_part = cache.shape[2]
    head_count = model_width // HD
    prompt_own = pre_dev * part_rows
    own_rows = prompt_own + dec_part
    states = jnp.concatenate(
        [prompt_states.reshape(prompt_own, model_width), decode_states], axis=0
    )
    starts = lax.dynamic_slice_in_dim(prompt_starts, data_pos * pre_dev, pre_dev)
    slot_ids = data_pos * dec_dev + jnp.arange(dec_dev, dtype=jnp.int32)
    matches = decode_slots[None, :] == slot_ids[:, None]
    slot_length = jnp.sum(jnp.where(matches, decode_lengths[None, :], 0), axis=1)
    offsets = jnp.arange(group_len, dtype=jnp.int32)
    prompt_pos = starts[:, None] + offsets[None, :]
    own_prompt_pos = lax.dynamic_slice_in_dim(
        prompt_pos, tensor_pos * part_rows, part_rows, 1
    ).reshape(prompt_own)
    own_decode_pos = lax.dynamic_slice_in_dim(slot_length, tensor_pos * dec_part, dec_part)
    own_pos = jnp.concatenate([own_prompt_pos, own_decode_pos], axis=0)
    projected = spread(states, w_qkv)
    query_raw = projected[:, 0].astype(jnp.bfloat16)
    key_raw = projected[:, 1].astype(jnp.bfloat16)
    value_raw = projected[:, 2].astype(jnp.bfloat16)
    query_all, key_all, value_all = (
        lax.all_gather(query_raw, "tensor", axis=1, tiled=True),
        lax.all_gather(key_raw, "tensor", axis=1, tiled=True),
        lax.all_gather(value_raw, "tensor", axis=1, tiled=True),
    )
    key_own = lax.dynamic_slice_in_dim(key_all, tensor_pos * own_rows, own_rows, 0)
    value_own = lax.dynamic_slice_in_dim(value_all, tensor_pos * own_rows, own_rows, 0)
    query_prompt, query_decode = split_rows(query_all, tensors, pre_dev, part_rows)
    query_prompt = rotate(rms_scale(query_prompt.astype(jnp.float32), gains[0]), prompt_pos).astype(
        jnp.bfloat16
    )
    query_decode = rotate(
        rms_scale(query_decode.astype(jnp.float32), gains[0]), slot_length
    ).astype(jnp.bfloat16)
    key_new = rotate(rms_scale(key_own.astype(jnp.float32), gains[1]), own_pos).astype(jnp.bfloat16)
    scale_factor = HD ** (-0.5)
    cache_pos = tensor_pos * ctx_part + jnp.arange(ctx_part, dtype=jnp.int32)
    prompt_q = query_prompt.reshape(pre_dev, group_len, head_count, HD)
    prompt_keys = cache[0, :pre_dev].reshape(pre_dev, ctx_part, head_count, HD)
    prompt_values = cache[1, :pre_dev].reshape(pre_dev, ctx_part, head_count, HD)
    fresh_keys = key_new[:prompt_own].reshape(pre_dev, part_rows, head_count, HD)
    fresh_values = value_own[:prompt_own].reshape(pre_dev, part_rows, head_count, HD)
    cached_scores = jnp.einsum(
        "aihe,ajhe->ahij", prompt_q, prompt_keys, preferred_element_type=jnp.float32
    )
    fresh_scores = jnp.einsum(
        "aihe,ajhe->ahij", prompt_q, fresh_keys, preferred_element_type=jnp.float32
    )
    prompt_scores = jnp.concatenate([cached_scores, fresh_scores], axis=-1) * scale_factor
    key_offsets = tensor_pos * part_rows + jnp.arange(part_rows, dtype=jnp.int32)
    live_cached = jnp.broadcast_to(
        (cache_pos[None, :] < starts[:, None])[:, None, None, :], (pre_dev, 1, group_len, ctx_part)
    )
    live_fresh = jnp.broadcast_to(
        (key_offsets[None, :] <= offsets[:, None])[None, None], (pre_dev, 1, group_len, part_rows)
    )
    prompt_live = jnp.concatenate([live_cached, live_fresh], axis=-1)
    prompt_masked = jnp.where(prompt_live, prompt_scores, MASKED_SCORE)
    prompt_top = jnp.max(prompt_masked, axis=-1)
    decode_q = query_decode.reshape(dec_dev, head_count, HD)
    decode_keys = cache[0, pre_dev:].reshape(dec_dev, ctx_part, head_count, HD)
    decode_values = cache[1, pre_dev:].reshape(dec_dev, ctx_part, head_count, HD)
    own_keys = key_new[prompt_own:].reshape(dec_part, head_count, HD)
    own_values = value_own[prompt_own:].reshape(dec_part, head_count, HD)
    decode_cached = jnp.einsum(
        "she,sjhe->shj", decode_q, decode_keys, preferred_element_type=jnp.float32
    )
    decode_fresh = jnp.einsum(
        "she,jhe->shj", decode_q, own_keys, preferred_element_type=jnp.float32
    )
    decode_scores = jnp.concatenate([decode_cached, decode_fresh], axis=-1) * scale_factor
    live_slots = (cache_pos[None, :] < slot_length[:, None])[:, None, :]
    own_ids = tensor_pos * dec_part + jnp.arange(dec_part, dtype=jnp.int32)
    live_owned = (jnp.arange(dec_dev, dtype=jnp.int32)[:, None] == own_ids[None, :])[:, None, :]
    decode_live = jnp.concatenate([live_slots, live_owned], axis=-1)
    decode_masked = jnp.where(decode_live, decode_scores, MASKED_SCORE)
    decode_top = jnp.max(decode_masked, axis=-1)
    prompt_weights = jnp.where(prompt_live, jnp.exp(prompt_masked - prompt_top[..., None]), 0.0)
    prompt_total = jnp.sum(prompt_weights, axis=-1)
    prompt_probs = prompt_weights.astype(jnp.bfloat16)
    prompt_mixed = jnp.einsum(
        "ahij,ajhe->aihe",
        prompt_probs[..., :ctx_part],
        prompt_values,
        preferred_element_type=jnp.float32,
    )
    prompt_mixed = prompt_mixed + jnp.einsum(
        "ahij,ajhe->aihe",
        prompt_probs[..., ctx_part:],
        fresh_values,
        preferred_element_type=jnp.float32,
    )
    decode_weights = jnp.where(decode_live, jnp.exp(decode_masked - decode_top[..., None]), 0.0)
    decode_total = jnp.sum(decode_weights, axis=-1)
    decode_probs = decode_weights.astype(jnp.bfloat16)
    decode_mixed = jnp.einsum(
        "shj,sjhe->she",
        decode_probs[..., :ctx_part],
        decode_values,
        preferred_element_type=jnp.float32,
    )
    decode_mixed = decode_mixed + jnp.einsum(
        "shj,jhe->she", decode_probs[..., ctx_part:], own_values, preferred_element_type=jnp.float32
    )
    totals = join_rows(jnp.swapaxes(prompt_total, 1, 2), decode_total, tensors)
    mixed = join_rows(
        prompt_mixed.reshape(pre_dev, group_len, model_width),
        decode_mixed.reshape(dec_dev, model_width),
        tensors,
    )
    tops = join_rows(jnp.swapaxes(prompt_top, 1, 2), decode_top, tensors)
    got_tops, got_totals, got_mixed = (
        lax.all_to_all(tops, "tensor", split_axis=0, concat_axis=0, tiled=True),
        lax.all_to_all(totals, "tensor", split_axis=0, concat_axis=0, tiled=True),
        lax.all_to_all(mixed, "tensor", split_axis=0, concat_axis=0, tiled=True),
    )
    got_tops = got_tops.reshape(tensors, own_rows, head_count)
    got_totals = got_totals.reshape(tensors, own_rows, head_count)
    got_mixed = got_mixed.reshape(tensors, own_rows, head_count, HD)
    highest = jnp.max(got_tops, axis=0)
    factors = jnp.exp(got_tops - highest[None])
    total_all = jnp.sum(got_totals * factors, axis=0)
    shares = lax.optimization_barrier((got_mixed * factors[..., None]).astype(jnp.bfloat16))
    mixed_all = jnp.sum(shares.astype(jnp.float32), axis=0)
    attended_own = (
        (mixed_all / total_all[..., None]).reshape(own_rows, model_width).astype(jnp.bfloat16)
    )
    my_columns = lax.all_to_all(attended_own, "tensor", split_axis=1, concat_axis=0, tiled=True)
    attn_sum = collect(my_columns, w_out)
    hidden = (states.astype(jnp.float32) + rms_scale(attn_sum, gains[2])).astype(jnp.bfloat16)
    gate_up = spread(hidden, w_gate_up)
    activated = (jax.nn.silu(gate_up[:, 0]) * gate_up[:, 1]).astype(jnp.bfloat16)
    ffn_sum = collect(activated, w_down)
    output = (hidden.astype(jnp.float32) + rms_scale(ffn_sum, gains[3])).astype(jnp.bfloat16)
    prompt_out = output[:prompt_own].reshape(pre_dev, part_rows, model_width)
    everyone = lax.all_gather(output[prompt_own:], ("dp", "tensor"), axis=0, tiled=True)
    wanted = lax.dynamic_slice_in_dim(
        decode_slots, (data_pos * tensors + tensor_pos) * dec_part, dec_part
    )
    decode_out = jnp.take(everyone, wanted, axis=0)
    new_prompt_kv = jnp.stack([key_new[:prompt_own], value_own[:prompt_own]]).reshape(
        2, pre_dev, part_rows, model_width
    )
    new_decode_kv = jnp.stack([key_new[prompt_own:], value_own[prompt_own:]])
    return (prompt_out, decode_out, new_prompt_kv, new_decode_kv)


Z = 4
BLOCK_PAD = 16


def z_pairs(targets):
    return [(z * 2 + c, t * 2 + c) for z in range(Z) for t in targets(z) for c in range(2)]


CORE = [(i, i ^ 1) for i in range(2 * Z)]
UP = [z_pairs(lambda z, k=k: [z + 1] if k <= z < Z - 1 else []) for k in range(Z - 1)]
DOWN = [z_pairs(lambda z, k=k: [z - 1] if 0 < z <= Z - 1 - k else []) for k in range(Z - 1)]
TURN = [z_pairs(lambda z, k=k: [(z + k) % Z]) for k in range(1, Z)]
ENDS = z_pairs(lambda z: {0: [1], 3: [2]}.get(z, []))
RISE = [z_pairs(lambda z: [z + 1] if z < 2 else []), z_pairs(lambda z: [z + 1] if z < 3 else [])]
FALL = [z_pairs(lambda z: [z - 1] if z > 1 else []), z_pairs(lambda z: [z - 1] if z > 0 else [])]


def send(values, pairs):
    return lax.ppermute(values, "tensor", pairs)


def small_gather(values, chip, core):
    pair = jnp.stack([values, send(values, CORE)])
    pair = jnp.where(core == 0, pair, pair[::-1])
    chips = jnp.stack([pair] + [send(pair, TURN[k]) for k in range(Z - 1)])
    order = (chip - jnp.arange(Z, dtype=jnp.int32)) % Z
    return jnp.take(chips, order, axis=0).reshape((2 * Z,) + values.shape)


def small_sum(values):
    total = values + send(values, CORE)
    parts = [send(total, TURN[k]) for k in range(Z - 1)]
    return total + parts[1] + (parts[0] + parts[2])


def exchange(blocks, chip, core):
    return spread_chips(swap_cores(blocks, core), chip)


def swap_cores(blocks, core):
    mine = lax.dynamic_index_in_dim(blocks, core, 1, keepdims=False)
    other = lax.dynamic_index_in_dim(blocks, 1 - core, 1, keepdims=False)
    return jnp.stack([mine, send(other, CORE)], axis=1)


def spread_chips(both, chip):
    got = [lax.dynamic_index_in_dim(both, chip, 0, keepdims=False)]
    for k in range(1, Z):
        part = lax.dynamic_index_in_dim(both, (chip + k) % Z, 0, keepdims=False)
        got.append(send(part, TURN[k - 1]))
    return got


def data_gather(values, data_pos):
    first = jnp.stack([values, lax.ppermute(values, "dp", [(i, i ^ 1) for i in range(4)])])
    second = lax.ppermute(first, "dp", [(i, i ^ 2) for i in range(4)])
    both = jnp.concatenate([first, second])
    return jnp.take(both, jnp.arange(4, dtype=jnp.int32) ^ data_pos, axis=0)


def params(limit):
    return pltpu.CompilerParams(vmem_limit_bytes=limit * 2**20)


VMEM = pl.BlockSpec(memory_space=pltpu.VMEM)
SMEM = pl.BlockSpec(memory_space=pltpu.SMEM)
ANY = pl.BlockSpec(memory_space=pl.ANY)


def hold_kernel(*refs):
    pass


def hold(values, *others):
    return pl.pallas_call(
        hold_kernel,
        in_specs=[ANY] * (1 + len(others)),
        out_specs=ANY,
        out_shape=jax.ShapeDtypeStruct(values.shape, values.dtype),
        input_output_aliases={0: 0},
        compiler_params=params(4),
        name="hold",
    )(values, *others)


def project_kernel(where, xa, xb, w, *refs):
    prompt_out, decode_out, rows_out, stats_out, rows = refs[-5:]
    core = where[1]
    own = xa.shape[0]
    rows[core] = xa[...]
    rows[1 - core] = xb[...]
    rows_out[...] = rows[:, 128:]
    both = jnp.concatenate([rows[0], rows[1]], axis=0)
    line = lax.broadcasted_iota(jnp.int32, (8, 256), 0)
    stats = jnp.zeros((8, 2 * own), jnp.float32)
    for part in range(3):
        made = jnp.dot(both, w[part], preferred_element_type=jnp.float32)
        made = made.astype(jnp.bfloat16)
        cols = pl.ds(part * 256, 256)
        for c in range(2):
            prompt_out[0, c, :, cols] = made[c * own : c * own + 64]
            prompt_out[1, c, :, cols] = made[c * own + 64 : c * own + 128]
            decode_out[c, :, cols] = made[c * own + 128 : (c + 1) * own]
        if part < 2:
            wide = made.astype(jnp.float32)
            stats = stats + lax.dot_general(
                jnp.where(line == part, 1.0, 0.0),
                wide * wide,
                (((1,), (1,)), ((), ())),
                precision=lax.Precision.HIGHEST,
                preferred_element_type=jnp.float32,
            )
    stats_out[0] = stats


def project(where, xa, xb, w, buffers, tokens=()):
    own, width = xa.shape
    shapes = [
        jax.ShapeDtypeStruct((2, 8, 64, 768), jnp.bfloat16),
        jax.ShapeDtypeStruct((8, own - 128, 768), jnp.bfloat16),
        jax.ShapeDtypeStruct((8, own - 128, width), jnp.bfloat16),
        jax.ShapeDtypeStruct((Z, 8, 2 * own), jnp.float32),
    ]
    grid_spec = pltpu.PrefetchScalarGridSpec(
        num_scalar_prefetch=1,
        grid=(1,),
        in_specs=[VMEM] * 3 + [ANY] * (len(buffers) + len(tokens)),
        out_specs=[
            pl.BlockSpec((2, 2, 64, 768), lambda i, s: (0, s[0], 0, 0)),
            pl.BlockSpec((2, own - 128, 768), lambda i, s: (s[0], 0, 0)),
            pl.BlockSpec((2, own - 128, width), lambda i, s: (s[0], 0, 0)),
            pl.BlockSpec((1, 8, 2 * own), lambda i, s: (s[0], 0, 0)),
        ],
        scratch_shapes=[pltpu.VMEM((2, own, width), jnp.bfloat16)],
    )
    return pl.pallas_call(
        project_kernel,
        grid_spec=grid_spec,
        out_shape=shapes,
        input_output_aliases={4 + i: i for i in range(len(buffers))},
        compiler_params=params(20),
        cost_estimate=pl.CostEstimate(
            flops=4 * own * width * 768, bytes_accessed=4 * 2**20, transcendentals=0
        ),
        name="project",
    )(where, xa, xb, w, *buffers, *tokens)


def swap_pairs(values):
    lane = lax.broadcasted_iota(jnp.int32, values.shape, 1)
    after = pltpu.roll(values, values.shape[1] - 1, 1)
    before = pltpu.roll(values, 1, 1)
    return jnp.where(lane % 2 == 0, after, before)


def attend_kernel(
    prompt, starts, q, k, v, g0, g1, g2, g3, scales, gain, cosine, sine, cached_at, *refs
):
    out, key_out = refs[-2:]
    cached = [
        jnp.concatenate([g[r, kind, 0] for g in (g0, g1, g2, g3) for r in range(2)], axis=0)
        for kind in range(2)
    ]
    width = 8 * 256
    scale = lax.rsqrt(jnp.transpose(scales[0]) / width + EPSILON)
    cos_t, sin_t = cosine[0], sine[0]

    def turn(raw, which):
        val = raw[0].astype(jnp.float32) * scale[:, which : which + 1] * gain[which : which + 1, :]
        return (val * cos_t + swap_pairs(val) * sin_t).astype(jnp.bfloat16)

    queries = turn(q, 0)
    keys = turn(k, 1)
    key_out[0] = keys
    dims = (((1,), (1,)), ((), ()))
    factor = HD ** (-0.5)
    rows = queries.shape[0]
    old = lax.dot_general(queries, cached[0], dims, preferred_element_type=jnp.float32) * factor
    new = lax.dot_general(queries, keys, dims, preferred_element_type=jnp.float32) * factor
    live_old = cached_at[...] < starts[prompt]
    live_new = lax.broadcasted_iota(jnp.int32, (rows, rows), 1) <= lax.broadcasted_iota(
        jnp.int32, (rows, rows), 0
    )
    old = jnp.where(live_old, old, MASKED_SCORE)
    new = jnp.where(live_new, new, MASKED_SCORE)
    top = jnp.maximum(
        jnp.max(old, axis=1, keepdims=True), jnp.max(new, axis=1, keepdims=True)
    )
    old = jnp.exp(old - top)
    new = jnp.exp(new - top)
    total = jnp.sum(old, axis=1, keepdims=True) + jnp.sum(new, axis=1, keepdims=True)
    mixed = jnp.dot(old.astype(jnp.bfloat16), cached[1], preferred_element_type=jnp.float32)
    mixed = mixed + jnp.dot(new.astype(jnp.bfloat16), v[0], preferred_element_type=jnp.float32)
    out[0] = (mixed / total).astype(jnp.bfloat16)


def attend(prompt, starts, qkv, cached, scales, gain, cosine, sine, cached_at, buffers, tokens):
    group = qkv.shape[1]
    part = cached[0].shape[3]
    ctx = 8 * part
    head = lambda off: pl.BlockSpec((1, group, HD), lambda h, s: (prompt, 0, off + h))
    grid_spec = pltpu.PrefetchScalarGridSpec(
        num_scalar_prefetch=1,
        grid=(2,),
        in_specs=[
            head(0),
            head(2),
            head(4),
            *[pl.BlockSpec((2, 2, 1, part, HD), lambda h, s: (0, 0, prompt, 0, h))] * Z,
            pl.BlockSpec((1, 8, group), lambda h, s: (prompt, 0, 0)),
            pl.BlockSpec((2, HD), lambda h, s: (0, h)),
            pl.BlockSpec((1, group, HD), lambda h, s: (prompt, 0, 0)),
            pl.BlockSpec((1, group, HD), lambda h, s: (prompt, 0, 0)),
            pl.BlockSpec((1, ctx), lambda h, s: (0, 0)),
        ]
        + [ANY] * (len(buffers) + len(tokens)),
        out_specs=[head(0), head(0)],
    )
    made = jax.ShapeDtypeStruct((2, group, 2 * HD), jnp.bfloat16)
    return pl.pallas_call(
        functools.partial(attend_kernel, prompt),
        grid_spec=grid_spec,
        out_shape=[made, made],
        input_output_aliases={13 + i: i for i in range(len(buffers))},
        compiler_params=params(16),
        cost_estimate=pl.CostEstimate(
            flops=8 * group * (group + ctx) * HD,
            bytes_accessed=6 * 2**20,
            transcendentals=2 * group * (group + ctx),
        ),
        name="attend",
    )(starts, qkv, qkv, qkv, *cached, scales, gain, cosine, sine, cached_at, *buffers, *tokens)


def decode_kernel(lengths, q, gains, cosine, sine, *refs):
    caches = refs[:4]
    mixed, marks, queries = refs[4:]
    step = pl.program_id(0)
    heads = q.shape[1] // HD
    width = q.shape[1]
    ctx = caches[0].shape[2]
    count = 8

    @pl.when(step == 0)
    def _():
        val = q[...].astype(jnp.float32)
        val = val * lax.rsqrt(jnp.mean(val * val, axis=1, keepdims=True) + EPSILON)
        val = val * gains[0:1, :]
        cos_t = jnp.concatenate([cosine[...]] * heads, axis=1)
        sin_t = jnp.concatenate([sine[...]] * heads, axis=1)
        val = val * cos_t + swap_pairs(val) * sin_t
        queries[...] = val.astype(jnp.bfloat16).astype(jnp.float32)

    first = lengths[lengths.shape[0] - 1]
    shape = (heads, width)
    own_head = lax.broadcasted_iota(jnp.int32, shape, 1) // HD == lax.broadcasted_iota(
        jnp.int32, shape, 0
    )
    rows, limits = [], []
    for j in range(count):
        slot = step * count + j
        row = jnp.broadcast_to(queries[pl.ds(slot, 1), :], shape)
        rows.append(jnp.where(own_head, row, 0.0).astype(jnp.bfloat16))
        limits.append(jnp.broadcast_to(lengths[slot] - first, (heads, 1)))
    keys = jnp.concatenate([cache[0, j] for cache in caches for j in range(2)], axis=0)
    values = jnp.concatenate([cache[1, j] for cache in caches for j in range(2)], axis=0)
    scores = lax.dot_general(
        jnp.concatenate(rows, axis=0),
        keys,
        (((1,), (1,)), ((), ())),
        preferred_element_type=jnp.float32,
    ) * HD ** (-0.5)
    size = (count * heads, count * ctx)
    line = lax.broadcasted_iota(jnp.int32, size, 0) // heads
    at = lax.broadcasted_iota(jnp.int32, size, 1) - line * ctx
    live = (at >= 0) & (at < ctx) & (at < jnp.concatenate(limits, axis=0))
    scores = jnp.where(live, scores, MASKED_SCORE)
    top = jnp.max(scores, axis=1, keepdims=True)
    weights = jnp.where(live, jnp.exp(scores - top), 0.0)
    total = jnp.sum(weights, axis=1, keepdims=True)
    marks[0, :, 0:1] = top
    marks[0, :, 1:2] = total
    part = jnp.dot(weights.astype(jnp.bfloat16), values, preferred_element_type=jnp.float32)
    for j in range(count):
        mixed[j : j + 1, :] = jnp.sum(
            jnp.where(own_head, part[j * heads : (j + 1) * heads], 0.0), axis=0, keepdims=True
        )


def decode(lengths, q, gains, cosine, sine, cache, skip):
    slots, width = q.shape
    ctx = cache.shape[2]
    heads = width // HD
    steps = slots // 8
    whole = lambda shape: pl.BlockSpec(shape, lambda i, s: (0, 0))
    pair = lambda j: pl.BlockSpec(
        (2, 2, ctx, width), lambda i, s: (0, i * 4 + j + skip // 2, 0, 0)
    )
    grid_spec = pltpu.PrefetchScalarGridSpec(
        num_scalar_prefetch=1,
        grid=(steps,),
        in_specs=[
            whole(q.shape),
            whole(gains.shape),
            whole(cosine.shape),
            whole(sine.shape),
        ]
        + [pair(j) for j in range(4)],
        out_specs=[
            pl.BlockSpec((8, width), lambda i, s: (i, 0)),
            pl.BlockSpec((1, 8 * heads, 2), lambda i, s: (i, 0, 0)),
        ],
        scratch_shapes=[pltpu.VMEM(q.shape, jnp.float32)],
    )
    mixed, marks = pl.pallas_call(
        decode_kernel,
        grid_spec=grid_spec,
        out_shape=[
            jax.ShapeDtypeStruct((slots, width), jnp.float32),
            jax.ShapeDtypeStruct((steps, 8 * heads, 2), jnp.float32),
        ],
        compiler_params=params(52),
        cost_estimate=pl.CostEstimate(
            flops=4 * slots * 128 * ctx * width, bytes_accessed=13 * 2**20, transcendentals=0
        ),
        name="decode",
    )(lengths, q, gains, cosine, sine, cache, cache, cache, cache)
    marks = marks.reshape(slots, heads, 2)
    return mixed, marks[..., 0], marks[..., 1]


def assemble_kernel(core, own, other, out, sems):
    made = []
    for j in range(4):
        for k, part in enumerate((own, other)):
            col = pl.multiple_of(j * 512 + (core[0] ^ k) * 256, 256)
            made.append(
                pltpu.make_async_copy(
                    part.at[j], out.at[:, pl.ds(col, 256)], sems.at[2 * j + k]
                )
            )
    for copy in made:
        copy.start()
    for copy in made:
        copy.wait()


def assemble(core, own, other):
    rows = own.shape[1]
    return pl.pallas_call(
        assemble_kernel,
        in_specs=[SMEM, ANY, ANY],
        out_specs=ANY,
        out_shape=jax.ShapeDtypeStruct((rows, 8 * 256), jnp.bfloat16),
        scratch_shapes=[pltpu.SemaphoreType.DMA((8,))],
        compiler_params=params(4),
        cost_estimate=pl.CostEstimate(flops=0, bytes_accessed=17 * 2**20, transcendentals=0),
        name="assemble",
    )(core, own, other)


def mix_kernel(where, *refs):
    lines = refs[:8]
    att, w, dec, dec_x, gain, out, xs, sems = refs[8:]
    step = pl.program_id(0)
    core = where[Z]
    copies = [
        pltpu.make_async_copy(lines[i], xs.at[where[i // 2], core ^ (i % 2)], sems.at[i])
        for i in range(8)
    ]

    @pl.when(step == 0)
    def _():
        for copy in copies:
            copy.start()

    sides = []
    for c in range(2):
        for p in range(2):
            sides.append(
                jnp.concatenate([att[k, p, c * 64 : (c + 1) * 64] for k in range(8)], axis=1)
            )
        sides.append(dec[c])
    rows = jnp.concatenate(sides, axis=0)
    total = jnp.dot(rows, w[...], preferred_element_type=jnp.float32)

    @pl.when(step == 0)
    def _():
        for copy in copies:
            copy.wait()

    inv = lax.rsqrt(jnp.mean(total * total, axis=1, keepdims=True) + EPSILON)
    total = total * inv * gain[2:3, :]
    per = 128 + BLOCK_PAD
    for c in range(2):
        base = c * per
        out[c, :128] = (
            xs[step, c, :128].astype(jnp.float32) + total[base : base + 128]
        ).astype(jnp.bfloat16)
        out[c, 128:] = (
            dec_x[c].astype(jnp.float32) + total[base + 128 : base + per]
        ).astype(jnp.bfloat16)


def mix(where, lines, att, w, dec, dec_x, gains):
    width = w.shape[1]
    return pl.pallas_call(
        mix_kernel,
        grid=(Z,),
        in_specs=[SMEM]
        + [ANY] * 8
        + [
            pl.BlockSpec((8, 2, 128, 256), lambda i: (0, 0, i, 0)),
            VMEM,
            pl.BlockSpec((2, BLOCK_PAD, width), lambda i: (i, 0, 0)),
            pl.BlockSpec((2, BLOCK_PAD, width), lambda i: (i, 0, 0)),
            pl.BlockSpec(gains.shape, lambda i: (0, 0)),
        ],
        out_specs=pl.BlockSpec((2, 128 + BLOCK_PAD, width), lambda i: (i, 0, 0)),
        out_shape=jax.ShapeDtypeStruct((8, 128 + BLOCK_PAD, width), jnp.bfloat16),
        scratch_shapes=[
            pltpu.VMEM((Z, 2) + lines[0].shape, jnp.bfloat16),
            pltpu.SemaphoreType.DMA((8,)),
        ],
        compiler_params=params(18),
        cost_estimate=pl.CostEstimate(
            flops=2 * 8 * 144 * width * width, bytes_accessed=22 * 2**20, transcendentals=0
        ),
        name="mix",
    )(where, *lines, att, w, dec, dec_x, gains)


def deliver_kernel(where, a, b, c, d, prompt_out, decode_out):
    for k, part in enumerate((a, b, c, d)):
        for r in range(2):
            cols = pl.ds(pl.multiple_of(where[2 * k + r] * 256, 256), 256)
            for kind in range(2):
                block = part[r, kind]
                prompt_out[kind, :, cols] = block[:128]
                decode_out[kind, :, cols] = block[128:]


def deliver(where, came, width):
    own = came[0].shape[2]
    return pl.pallas_call(
        deliver_kernel,
        in_specs=[SMEM] + [VMEM] * 4,
        out_specs=[VMEM, VMEM],
        out_shape=[
            jax.ShapeDtypeStruct((2, 128, width), jnp.bfloat16),
            jax.ShapeDtypeStruct((2, own - 128, width), jnp.bfloat16),
        ],
        compiler_params=params(8),
        cost_estimate=pl.CostEstimate(flops=0, bytes_accessed=2**22, transcendentals=0),
        name="deliver",
    )(where, *came)


def forward_kernel(where, hidden, wgu, wd, *refs):
    mine, other, acc = refs[-3:]
    per = hidden.shape[1]
    rows = hidden[pl.ds(where[0] * 2, 2)].reshape(2 * per, hidden.shape[2])
    half = wd.shape[0] // 2
    total = None
    for i in range(2):
        cols = pl.ds(i * half, half)
        gate = jnp.dot(rows, wgu[0, :, cols], preferred_element_type=jnp.float32)
        up = jnp.dot(rows, wgu[1, :, cols], preferred_element_type=jnp.float32)
        act = (gate / (1.0 + jnp.exp(-gate)) * up).astype(jnp.bfloat16)
        part = jnp.dot(act, wd[cols], preferred_element_type=jnp.float32)
        total = part if total is None else total + part
    acc[...] = total.reshape(acc.shape)
    core = where[1]
    mine[...] = acc[core, : mine.shape[0]].astype(jnp.bfloat16)
    other[...] = acc[1 - core, : mine.shape[0]].astype(jnp.bfloat16)


def forward(where, hidden, wgu, wd, rows, tokens):
    per, width = hidden.shape[1:]
    made = jax.ShapeDtypeStruct((rows, width), jnp.bfloat16)
    return pl.pallas_call(
        forward_kernel,
        in_specs=[SMEM, VMEM, VMEM, VMEM] + [ANY] * len(tokens),
        out_specs=[VMEM, VMEM],
        out_shape=[made, made],
        scratch_shapes=[pltpu.VMEM((2, per, width), jnp.float32)],
        compiler_params=params(12),
        cost_estimate=pl.CostEstimate(
            flops=12 * per * width * wd.shape[0], bytes_accessed=4 * 2**20, transcendentals=0
        ),
        name="forward",
    )(where, hidden, wgu, wd, *tokens)


def tables(positions):
    lanes = jnp.arange(HD, dtype=jnp.int32)
    freq_index = (lanes // 2).astype(jnp.float32)
    inv_freq = jnp.power(ROPE_BASE, -2.0 * freq_index / HD)
    angles = positions.astype(jnp.float32)[..., None] * inv_freq
    sign = jnp.where(lanes % 2 == 0, -1.0, 1.0)
    return jnp.cos(angles), jnp.sin(angles) * sign


def turn_kernel(where, a, b, up, down, up_out, down_out):
    chip = where[0]
    one, two = a[...].astype(jnp.float32), b[...].astype(jnp.float32)
    up_out[...] = (jnp.where(chip == 1, one, two) + up[...]).astype(jnp.bfloat16)
    down_out[...] = (jnp.where(chip == 2, one, two) + down[...]).astype(jnp.bfloat16)


def turn_sums(where, a, b, up, down):
    made = jax.ShapeDtypeStruct(a.shape, a.dtype)
    return pl.pallas_call(
        turn_kernel,
        in_specs=[SMEM] + [VMEM] * 4,
        out_specs=[VMEM, VMEM],
        out_shape=[made, made],
        compiler_params=params(10),
        cost_estimate=pl.CostEstimate(flops=0, bytes_accessed=2**22, transcendentals=0),
        name="turn_sums",
    )(where, a, b, up, down)


def narrow_sum(*terms):
    total = terms[0].astype(jnp.float32)
    for term in terms[1:]:
        total = total + term.astype(jnp.float32)
    return total.astype(jnp.bfloat16)


def after(values, *others):
    return lax.optimization_barrier((values,) + others)[0]


def local_heads(
    prompt_states,
    decode_states,
    cache,
    prompt_starts,
    decode_lengths,
    decode_slots,
    w_qkv,
    w_out,
    w_gate_up,
    w_down,
    gains,
):
    place = lax.axis_index("tensor")
    chip, core = place // 2, place % 2
    data_pos = lax.axis_index("dp")
    pre_dev, part_rows, width = prompt_states.shape
    dec_part = decode_states.shape[0]
    group = part_rows * 8
    dec_dev = dec_part * 8
    ctx_part = cache.shape[2]
    heads = width // HD
    own_rows = pre_dev * part_rows + dec_part
    states = jnp.concatenate(
        [prompt_states.reshape(pre_dev * part_rows, width), decode_states], axis=0
    )
    starts = lax.dynamic_slice_in_dim(prompt_starts, data_pos * pre_dev, pre_dev)
    slot_ids = data_pos * dec_dev + jnp.arange(dec_dev, dtype=jnp.int32)
    matches = decode_slots[None, :] == slot_ids[:, None]
    slot_length = jnp.sum(jnp.where(matches, decode_lengths[None, :], 0), axis=1)
    prompt_pos = starts[:, None] + jnp.arange(group, dtype=jnp.int32)[None, :]
    cos_p, sin_p = tables(prompt_pos)
    cos_d, sin_d = tables(slot_length)
    my_gains = lax.dynamic_slice_in_dim(gains[:2], place * 256, 256, 1)

    chips_at = (chip - jnp.arange(Z, dtype=jnp.int32)) % Z
    blocks_at = jnp.stack([chips_at * 2 + core, chips_at * 2 + 1 - core], axis=1).astype(jnp.int32)
    low, end = chip < 2, (chip == 0) | (chip == Z - 1)

    lines = []

    def add_block(line, source, buffers, *tokens):
        at = jnp.stack([source, core]).astype(jnp.int32)
        other = send(line, CORE)
        lines.extend([line, other])
        return project(at, line, other, w_qkv, buffers, tokens)

    rise1, fall1 = send(states, UP[0]), send(states, DOWN[0])
    prompt_cache = cache[:, :pre_dev]
    prompt_cache = jnp.stack(
        [
            jnp.stack(
                [prompt_cache[..., (2 * z + c) * 256 : (2 * z + c + 1) * 256] for c in range(2)]
            )
            for z in range(Z)
        ]
    )
    cache_pair = swap_cores(prompt_cache, core)
    buffers = add_block(states, chip, (), cache_pair)
    rise2, fall2 = send(rise1, UP[1]), send(fall1, DOWN[1])
    line = jnp.where(chip % 2 == 0, fall1, rise1)
    buffers = add_block(line, chip ^ 1, buffers)
    rise2, fall2, *buffers = lax.optimization_barrier((rise2, fall2, *buffers))
    rise3, fall3 = send(rise2, UP[2]), send(fall2, DOWN[2])
    line = jnp.where(low, jnp.where(end, fall2, fall1), jnp.where(end, rise2, rise1))
    buffers = add_block(line, jnp.where(low, 2, 1), buffers)
    rise3, fall3, *buffers = lax.optimization_barrier((rise3, fall3, *buffers))
    line = jnp.where(low, jnp.where(end, fall3, fall2), jnp.where(end, rise3, rise2))
    buffers = add_block(line, jnp.where(low, 3, 0), buffers)
    prompt_raw, decode_raw, dec_x, stats = buffers
    prompt_raw = prompt_raw.reshape(pre_dev, group, 768)
    decode_raw = decode_raw.reshape(dec_dev, 768)

    cached_at = (
        blocks_at.reshape(8, 1) * ctx_part + jnp.arange(ctx_part, dtype=jnp.int32)[None, :]
    ).reshape(1, 8 * ctx_part)

    share = width // 4
    w_share = lax.dynamic_slice_in_dim(w_out, data_pos * share, share, 1)
    w_share = w_share.reshape(1, w_out.shape[0], 2, share // 2)
    w_pair = swap_cores(jnp.transpose(w_share, (0, 2, 1, 3)), core)[0]
    w_pair = jnp.where(core == 0, w_pair, w_pair[::-1])
    lanes = [[2 * z + c for z in range(Z)] for c in range(2)]
    w_line = lax.all_gather(w_pair, "tensor", axis=0, axis_index_groups=lanes)
    w_line = hold(w_line, stats)
    w_own = lax.all_gather(w_line.reshape(width, share // 2), "dp", axis=0)
    w_full = assemble(core[None].astype(jnp.int32), w_own, send(w_own, CORE))

    stats = small_sum(stats).reshape(Z, 8, 2, own_rows)
    prompt_stats = stats[..., : own_rows - dec_part].reshape(Z, 8, 2, pre_dev, part_rows)
    prompt_stats = jnp.transpose(prompt_stats, (3, 1, 0, 2, 4)).reshape(pre_dev, 8, group)
    dec_stats = jnp.transpose(stats[..., own_rows - dec_part :], (0, 2, 3, 1)).reshape(dec_dev, 8)
    dec_scales = lax.rsqrt(dec_stats / width + EPSILON)
    def turn(raw, scale, gain):
        val = raw.astype(jnp.float32) * scale * gain
        even = jnp.arange(val.shape[1]) % 2 == 0
        swapped = jnp.where(even, jnp.roll(val, -1, axis=1), jnp.roll(val, 1, axis=1))
        cos_t = jnp.concatenate([cos_d] * 2, axis=1)
        sin_t = jnp.concatenate([sin_d] * 2, axis=1)
        return (val * cos_t + swapped * sin_t).astype(jnp.bfloat16).reshape(-1, 2, HD)

    query_mine = turn(decode_raw[:, :256], dec_scales[:, :1], my_gains[0])
    key_mine = turn(decode_raw[:, 256:512], dec_scales[:, 1:2], my_gains[1])
    value_mine = decode_raw[:, 512:].reshape(dec_dev, 2, HD)
    query_all = small_gather(decode_raw[:, :256], chip, core)
    query_all = jnp.swapaxes(query_all, 0, 1).reshape(dec_dev, width)
    got = spread_chips(hold(cache_pair, query_all), chip)
    scale_factor = HD ** (-0.5)
    lengths = jnp.concatenate([slot_length, (place * ctx_part)[None]]).astype(jnp.int32)
    mixed, tops, sums = decode(lengths, query_all, gains, cos_d, sin_d, cache, pre_dev)
    parts = jnp.concatenate(
        [
            jnp.transpose(mixed.reshape(dec_dev, 8, 256), (1, 0, 2)),
            jnp.transpose(tops.reshape(dec_dev, 8, 2), (1, 0, 2)),
            jnp.transpose(sums.reshape(dec_dev, 8, 2), (1, 0, 2)),
        ],
        axis=-1,
    )
    parts = swap_cores(parts.reshape(Z, 2, dec_dev, 260), core)
    arrived = spread_chips(parts, chip)
    made = ()
    for prompt, tokens in enumerate(((parts,), arrived)):
        made = attend(
            prompt,
            starts,
            prompt_raw,
            got,
            prompt_stats,
            my_gains,
            cos_p,
            sin_p,
            cached_at,
            made,
            tokens,
        )
    attended, key_new = made
    arrived = jnp.stack(arrived).reshape(8, dec_dev, 260)
    got_mixed = arrived[..., :256].reshape(8, dec_dev, 2, HD)
    got_tops, got_sums = arrived[..., 256:258], arrived[..., 258:]
    own_score = (
        jnp.sum(query_mine.astype(jnp.float32) * key_mine.astype(jnp.float32), axis=-1)
        * scale_factor
    )
    highest = jnp.maximum(jnp.max(got_tops, axis=0), own_score)
    factors = jnp.exp(got_tops - highest[None])
    own_weight = jnp.exp(own_score - highest)
    total = jnp.sum(got_sums * factors, axis=0) + own_weight
    summed = jnp.sum(got_mixed * factors[..., None], axis=0)
    summed = summed + own_weight.astype(jnp.bfloat16).astype(jnp.float32)[
        ..., None
    ] * value_mine.astype(jnp.float32)
    dec_attended = (summed / total[..., None]).reshape(dec_dev, 256).astype(jnp.bfloat16)
    wanted = lax.dynamic_slice_in_dim(decode_slots, data_pos * dec_dev, dec_dev)
    by_request = jnp.take(
        data_gather(dec_attended, data_pos).reshape(4 * dec_dev, 256), wanted, axis=0
    )
    pad = lambda v: jnp.pad(
        v.reshape(8, dec_part, width), ((0, 0), (0, BLOCK_PAD - dec_part), (0, 0))
    )
    dec_rows = small_gather(by_request, chip, core)
    dec_rows = pad(jnp.swapaxes(dec_rows, 0, 1).reshape(dec_dev, width))
    dec_x = after(dec_x.reshape(dec_dev, width), attended)
    dec_x = data_gather(dec_x, data_pos)
    dec_x = pad(jnp.take(dec_x.reshape(4 * dec_dev, width), wanted, axis=0))

    fresh = jnp.stack([key_new, prompt_raw[:, :, 512:]])
    fresh = fresh.reshape(2, pre_dev, 8, part_rows, 256)
    fresh = jnp.transpose(fresh, (2, 0, 1, 3, 4)).reshape(8, 2, pre_dev * part_rows, 256)
    fresh_dec = jnp.stack([key_mine.reshape(dec_dev, 256), decode_raw[:, 512:]])
    fresh_dec = jnp.transpose(fresh_dec.reshape(2, 8, dec_part, 256), (1, 0, 2, 3))
    fresh = jnp.concatenate([fresh, fresh_dec], axis=2)
    fresh_pair = swap_cores(fresh.reshape(Z, 2, 2, own_rows, 256), core)

    att = lax.all_gather(attended, "tensor", axis=0)
    fresh_pair = after(fresh_pair, att)
    kv_came = spread_chips(fresh_pair, chip)
    where = jnp.stack(
        [chip, chip ^ 1, jnp.where(low, 2, 1), jnp.where(low, 3, 0), core]
    ).astype(jnp.int32)
    hidden = mix(where, lines, att, w_full, dec_rows, dec_x, gains)

    orders = jnp.array([[3, 2, 1, 0], [3, 2, 0, 1], [0, 1, 3, 2], [0, 1, 2, 3]], jnp.int32)
    order = lax.dynamic_index_in_dim(orders, chip, 0, keepdims=False)
    sums = []
    for k in range(Z):
        at = jnp.stack([order[k], core]).astype(jnp.int32)
        tokens = [kv_came, sums, (), ()][k]
        mine, other = forward(at, hidden, w_gate_up, w_down, own_rows, tokens)
        sums.append(narrow_sum(mine, send(other, CORE)))
    came = after(send(sums[0], ENDS), mine)
    is_end = (chip == 0) | (chip == 3)
    load = narrow_sum(jnp.where(is_end, sums[1], sums[0]), came)
    up, down = send(load, RISE[0]), send(load, FALL[0])
    up, down = turn_sums(chip[None].astype(jnp.int32), sums[1], sums[2], up, down)
    up, down = send(up, RISE[1]), send(down, FALL[1])
    ffn_sum = sums[3].astype(jnp.float32) + up.astype(jnp.float32) + down.astype(jnp.float32)
    hidden_own = lax.dynamic_index_in_dim(hidden, place, 0, keepdims=False)[:own_rows]
    output = (hidden_own.astype(jnp.float32) + rms_scale(ffn_sum, gains[3])).astype(jnp.bfloat16)
    prompt_out = output[: own_rows - dec_part].reshape(pre_dev, part_rows, width)
    decode_out = output[own_rows - dec_part :]

    new_prompt_kv, new_decode_kv = deliver(blocks_at.reshape(8), kv_came, width)
    new_prompt_kv = new_prompt_kv.reshape(2, pre_dev, part_rows, width)
    return (prompt_out, decode_out, new_prompt_kv, new_decode_kv)


def fits_heads(mesh):
    return mesh.shape["tensor"] == 2 * Z and mesh.shape["dp"] == 4


def solution(mesh):
    in_specs = (
        P("dp", "tensor", None),
        P(("dp", "tensor"), None),
        P(None, "dp", "tensor", None),
        P(),
        P(),
        P(),
        P(None, None, "tensor"),
        P("tensor", None),
        P(None, None, "tensor"),
        P("tensor", None),
        P(),
    )
    out_specs = (
        P("dp", "tensor", None),
        P(("dp", "tensor"), None),
        P(None, "dp", "tensor", None),
        P(None, ("dp", "tensor"), None),
    )
    body = local_heads if fits_heads(mesh) else local
    return jax.shard_map(body, mesh=mesh, in_specs=in_specs, out_specs=out_specs, check_vma=False)
```

```python
import functools

import jax
import jax.numpy as jnp
from jax import lax
from jax.experimental import pallas as pl
from jax.experimental.pallas import tpu as pltpu
from jax.sharding import PartitionSpec as P

HD = 128


EPSILON = 1e-06
ROPE_BASE = 500000.0
MASKED_SCORE = -1e30


def rms_scale(values, gain_vec):
    return (
        values * lax.rsqrt(jnp.mean(values * values, axis=-1, keepdims=True) + EPSILON) * gain_vec
    )


def rotate(values, positions):
    full_shape = values.shape
    paired = values.reshape(full_shape[:-1] + (full_shape[-1] // HD, HD // 2, 2))
    freq_index = jnp.arange(HD // 2, dtype=jnp.float32)
    inv_freq = jnp.power(ROPE_BASE, -2.0 * freq_index / HD)
    angles = positions.astype(jnp.float32)[..., None, None] * inv_freq
    cosine = jnp.cos(angles)
    sine_values = jnp.sin(angles)
    even_part = paired[..., 0]
    odd_part = paired[..., 1]
    turned = jnp.stack(
        [even_part * cosine - odd_part * sine_values, even_part * sine_values + odd_part * cosine],
        axis=-1,
    )
    return turned.reshape(full_shape)


def split_rows(stacked, tensors, pre_dev, part_rows):
    tail_shape = stacked.shape[1:]
    per_device = stacked.shape[0] // tensors
    device_grid = stacked.reshape((tensors, per_device) + tail_shape)
    prompt_part = device_grid[:, : pre_dev * part_rows].reshape(
        (tensors, pre_dev, part_rows) + tail_shape
    )
    prompt_part = jnp.swapaxes(prompt_part, 0, 1).reshape(
        (pre_dev, tensors * part_rows) + tail_shape
    )
    decode_part = device_grid[:, pre_dev * part_rows :].reshape((-1,) + tail_shape)
    return (prompt_part, decode_part)


def join_rows(prompt_part, decode_part, tensors):
    pre_dev = prompt_part.shape[0]
    part_rows = prompt_part.shape[1] // tensors
    tail_shape = prompt_part.shape[2:]
    leading = jnp.swapaxes(prompt_part.reshape((pre_dev, tensors, part_rows) + tail_shape), 0, 1)
    leading = leading.reshape((tensors, pre_dev * part_rows) + tail_shape)
    trailing = decode_part.reshape((tensors, -1) + tail_shape)
    return jnp.concatenate([leading, trailing], axis=1).reshape((-1,) + tail_shape)


def spread(local_rows, weights):
    return jnp.einsum(
        "rd,kdc->rkc",
        lax.all_gather(local_rows, "tensor", axis=0, tiled=True),
        weights,
        preferred_element_type=jnp.float32,
    )


def collect(operand, weights):
    return lax.psum_scatter(
        jnp.dot(operand, weights, preferred_element_type=jnp.float32).astype(jnp.bfloat16),
        "tensor",
        scatter_dimension=0,
        tiled=True,
    ).astype(jnp.float32)


def local(
    prompt_states,
    decode_states,
    cache,
    prompt_starts,
    decode_lengths,
    decode_slots,
    w_qkv,
    w_out,
    w_gate_up,
    w_down,
    gains,
):
    tensors = lax.axis_size("tensor")
    tensor_pos = lax.axis_index("tensor")
    data_pos = lax.axis_index("dp")
    pre_dev, part_rows, model_width = prompt_states.shape
    dec_part = decode_states.shape[0]
    group_len = part_rows * tensors
    dec_dev = dec_part * tensors
    ctx_part = cache.shape[2]
    head_count = model_width // HD
    prompt_own = pre_dev * part_rows
    own_rows = prompt_own + dec_part
    states = jnp.concatenate(
        [prompt_states.reshape(prompt_own, model_width), decode_states], axis=0
    )
    starts = lax.dynamic_slice_in_dim(prompt_starts, data_pos * pre_dev, pre_dev)
    slot_ids = data_pos * dec_dev + jnp.arange(dec_dev, dtype=jnp.int32)
    matches = decode_slots[None, :] == slot_ids[:, None]
    slot_length = jnp.sum(jnp.where(matches, decode_lengths[None, :], 0), axis=1)
    offsets = jnp.arange(group_len, dtype=jnp.int32)
    prompt_pos = starts[:, None] + offsets[None, :]
    own_prompt_pos = lax.dynamic_slice_in_dim(
        prompt_pos, tensor_pos * part_rows, part_rows, 1
    ).reshape(prompt_own)
    own_decode_pos = lax.dynamic_slice_in_dim(slot_length, tensor_pos * dec_part, dec_part)
    own_pos = jnp.concatenate([own_prompt_pos, own_decode_pos], axis=0)
    projected = spread(states, w_qkv)
    query_raw = projected[:, 0].astype(jnp.bfloat16)
    key_raw = projected[:, 1].astype(jnp.bfloat16)
    value_raw = projected[:, 2].astype(jnp.bfloat16)
    query_all, key_all, value_all = (
        lax.all_gather(query_raw, "tensor", axis=1, tiled=True),
        lax.all_gather(key_raw, "tensor", axis=1, tiled=True),
        lax.all_gather(value_raw, "tensor", axis=1, tiled=True),
    )
    key_own = lax.dynamic_slice_in_dim(key_all, tensor_pos * own_rows, own_rows, 0)
    value_own = lax.dynamic_slice_in_dim(value_all, tensor_pos * own_rows, own_rows, 0)
    query_prompt, query_decode = split_rows(query_all, tensors, pre_dev, part_rows)
    query_prompt = rotate(rms_scale(query_prompt.astype(jnp.float32), gains[0]), prompt_pos).astype(
        jnp.bfloat16
    )
    query_decode = rotate(
        rms_scale(query_decode.astype(jnp.float32), gains[0]), slot_length
    ).astype(jnp.bfloat16)
    key_new = rotate(rms_scale(key_own.astype(jnp.float32), gains[1]), own_pos).astype(jnp.bfloat16)
    scale_factor = HD ** (-0.5)
    cache_pos = tensor_pos * ctx_part + jnp.arange(ctx_part, dtype=jnp.int32)
    prompt_q = query_prompt.reshape(pre_dev, group_len, head_count, HD)
    prompt_keys = cache[0, :pre_dev].reshape(pre_dev, ctx_part, head_count, HD)
    prompt_values = cache[1, :pre_dev].reshape(pre_dev, ctx_part, head_count, HD)
    fresh_keys = key_new[:prompt_own].reshape(pre_dev, part_rows, head_count, HD)
    fresh_values = value_own[:prompt_own].reshape(pre_dev, part_rows, head_count, HD)
    cached_scores = jnp.einsum(
        "aihe,ajhe->ahij", prompt_q, prompt_keys, preferred_element_type=jnp.float32
    )
    fresh_scores = jnp.einsum(
        "aihe,ajhe->ahij", prompt_q, fresh_keys, preferred_element_type=jnp.float32
    )
    prompt_scores = jnp.concatenate([cached_scores, fresh_scores], axis=-1) * scale_factor
    key_offsets = tensor_pos * part_rows + jnp.arange(part_rows, dtype=jnp.int32)
    live_cached = jnp.broadcast_to(
        (cache_pos[None, :] < starts[:, None])[:, None, None, :], (pre_dev, 1, group_len, ctx_part)
    )
    live_fresh = jnp.broadcast_to(
        (key_offsets[None, :] <= offsets[:, None])[None, None], (pre_dev, 1, group_len, part_rows)
    )
    prompt_live = jnp.concatenate([live_cached, live_fresh], axis=-1)
    prompt_masked = jnp.where(prompt_live, prompt_scores, MASKED_SCORE)
    prompt_top = jnp.max(prompt_masked, axis=-1)
    decode_q = query_decode.reshape(dec_dev, head_count, HD)
    decode_keys = cache[0, pre_dev:].reshape(dec_dev, ctx_part, head_count, HD)
    decode_values = cache[1, pre_dev:].reshape(dec_dev, ctx_part, head_count, HD)
    own_keys = key_new[prompt_own:].reshape(dec_part, head_count, HD)
    own_values = value_own[prompt_own:].reshape(dec_part, head_count, HD)
    decode_cached = jnp.einsum(
        "she,sjhe->shj", decode_q, decode_keys, preferred_element_type=jnp.float32
    )
    decode_fresh = jnp.einsum(
        "she,jhe->shj", decode_q, own_keys, preferred_element_type=jnp.float32
    )
    decode_scores = jnp.concatenate([decode_cached, decode_fresh], axis=-1) * scale_factor
    live_slots = (cache_pos[None, :] < slot_length[:, None])[:, None, :]
    own_ids = tensor_pos * dec_part + jnp.arange(dec_part, dtype=jnp.int32)
    live_owned = (jnp.arange(dec_dev, dtype=jnp.int32)[:, None] == own_ids[None, :])[:, None, :]
    decode_live = jnp.concatenate([live_slots, live_owned], axis=-1)
    decode_masked = jnp.where(decode_live, decode_scores, MASKED_SCORE)
    decode_top = jnp.max(decode_masked, axis=-1)
    prompt_weights = jnp.where(prompt_live, jnp.exp(prompt_masked - prompt_top[..., None]), 0.0)
    prompt_total = jnp.sum(prompt_weights, axis=-1)
    prompt_probs = prompt_weights.astype(jnp.bfloat16)
    prompt_mixed = jnp.einsum(
        "ahij,ajhe->aihe",
        prompt_probs[..., :ctx_part],
        prompt_values,
        preferred_element_type=jnp.float32,
    )
    prompt_mixed = prompt_mixed + jnp.einsum(
        "ahij,ajhe->aihe",
        prompt_probs[..., ctx_part:],
        fresh_values,
        preferred_element_type=jnp.float32,
    )
    decode_weights = jnp.where(decode_live, jnp.exp(decode_masked - decode_top[..., None]), 0.0)
    decode_total = jnp.sum(decode_weights, axis=-1)
    decode_probs = decode_weights.astype(jnp.bfloat16)
    decode_mixed = jnp.einsum(
        "shj,sjhe->she",
        decode_probs[..., :ctx_part],
        decode_values,
        preferred_element_type=jnp.float32,
    )
    decode_mixed = decode_mixed + jnp.einsum(
        "shj,jhe->she", decode_probs[..., ctx_part:], own_values, preferred_element_type=jnp.float32
    )
    totals = join_rows(jnp.swapaxes(prompt_total, 1, 2), decode_total, tensors)
    mixed = join_rows(
        prompt_mixed.reshape(pre_dev, group_len, model_width),
        decode_mixed.reshape(dec_dev, model_width),
        tensors,
    )
    tops = join_rows(jnp.swapaxes(prompt_top, 1, 2), decode_top, tensors)
    got_tops, got_totals, got_mixed = (
        lax.all_to_all(tops, "tensor", split_axis=0, concat_axis=0, tiled=True),
        lax.all_to_all(totals, "tensor", split_axis=0, concat_axis=0, tiled=True),
        lax.all_to_all(mixed, "tensor", split_axis=0, concat_axis=0, tiled=True),
    )
    got_tops = got_tops.reshape(tensors, own_rows, head_count)
    got_totals = got_totals.reshape(tensors, own_rows, head_count)
    got_mixed = got_mixed.reshape(tensors, own_rows, head_count, HD)
    highest = jnp.max(got_tops, axis=0)
    factors = jnp.exp(got_tops - highest[None])
    total_all = jnp.sum(got_totals * factors, axis=0)
    shares = lax.optimization_barrier((got_mixed * factors[..., None]).astype(jnp.bfloat16))
    mixed_all = jnp.sum(shares.astype(jnp.float32), axis=0)
    attended_own = (
        (mixed_all / total_all[..., None]).reshape(own_rows, model_width).astype(jnp.bfloat16)
    )
    my_columns = lax.all_to_all(attended_own, "tensor", split_axis=1, concat_axis=0, tiled=True)
    attn_sum = collect(my_columns, w_out)
    hidden = (states.astype(jnp.float32) + rms_scale(attn_sum, gains[2])).astype(jnp.bfloat16)
    gate_up = spread(hidden, w_gate_up)
    activated = (jax.nn.silu(gate_up[:, 0]) * gate_up[:, 1]).astype(jnp.bfloat16)
    ffn_sum = collect(activated, w_down)
    output = (hidden.astype(jnp.float32) + rms_scale(ffn_sum, gains[3])).astype(jnp.bfloat16)
    prompt_out = output[:prompt_own].reshape(pre_dev, part_rows, model_width)
    everyone = lax.all_gather(output[prompt_own:], ("dp", "tensor"), axis=0, tiled=True)
    wanted = lax.dynamic_slice_in_dim(
        decode_slots, (data_pos * tensors + tensor_pos) * dec_part, dec_part
    )
    decode_out = jnp.take(everyone, wanted, axis=0)
    new_prompt_kv = jnp.stack([key_new[:prompt_own], value_own[:prompt_own]]).reshape(
        2, pre_dev, part_rows, model_width
    )
    new_decode_kv = jnp.stack([key_new[prompt_own:], value_own[prompt_own:]])
    return (prompt_out, decode_out, new_prompt_kv, new_decode_kv)


Z = 4
BLOCK_PAD = 16


def z_pairs(targets):
    return [(z * 2 + c, t * 2 + c) for z in range(Z) for t in targets(z) for c in range(2)]


CORE = [(i, i ^ 1) for i in range(2 * Z)]
UP = [z_pairs(lambda z, k=k: [z + 1] if k <= z < Z - 1 else []) for k in range(Z - 1)]
DOWN = [z_pairs(lambda z, k=k: [z - 1] if 0 < z <= Z - 1 - k else []) for k in range(Z - 1)]
TURN = [z_pairs(lambda z, k=k: [(z + k) % Z]) for k in range(1, Z)]
ENDS = z_pairs(lambda z: {0: [1], 3: [2]}.get(z, []))
RISE = [z_pairs(lambda z: [z + 1] if z < 2 else []), z_pairs(lambda z: [z + 1] if z < 3 else [])]
FALL = [z_pairs(lambda z: [z - 1] if z > 1 else []), z_pairs(lambda z: [z - 1] if z > 0 else [])]


def send(values, pairs):
    return lax.ppermute(values, "tensor", pairs)


def small_gather(values, chip, core):
    pair = jnp.stack([values, send(values, CORE)])
    pair = jnp.where(core == 0, pair, pair[::-1])
    chips = jnp.stack([pair] + [send(pair, TURN[k]) for k in range(Z - 1)])
    order = (chip - jnp.arange(Z, dtype=jnp.int32)) % Z
    return jnp.take(chips, order, axis=0).reshape((2 * Z,) + values.shape)


def small_sum(values):
    total = values + send(values, CORE)
    parts = [send(total, TURN[k]) for k in range(Z - 1)]
    return total + parts[1] + (parts[0] + parts[2])


def exchange(blocks, chip, core):
    return spread_chips(swap_cores(blocks, core), chip)


def swap_cores(blocks, core):
    mine = lax.dynamic_index_in_dim(blocks, core, 1, keepdims=False)
    other = lax.dynamic_index_in_dim(blocks, 1 - core, 1, keepdims=False)
    return jnp.stack([mine, send(other, CORE)], axis=1)


def spread_chips(both, chip):
    got = [lax.dynamic_index_in_dim(both, chip, 0, keepdims=False)]
    for k in range(1, Z):
        part = lax.dynamic_index_in_dim(both, (chip + k) % Z, 0, keepdims=False)
        got.append(send(part, TURN[k - 1]))
    return got


def data_gather(values, data_pos):
    first = jnp.stack([values, lax.ppermute(values, "dp", [(i, i ^ 1) for i in range(4)])])
    second = lax.ppermute(first, "dp", [(i, i ^ 2) for i in range(4)])
    both = jnp.concatenate([first, second])
    return jnp.take(both, jnp.arange(4, dtype=jnp.int32) ^ data_pos, axis=0)


def params(limit):
    return pltpu.CompilerParams(vmem_limit_bytes=limit * 2**20)


VMEM = pl.BlockSpec(memory_space=pltpu.VMEM)
SMEM = pl.BlockSpec(memory_space=pltpu.SMEM)
ANY = pl.BlockSpec(memory_space=pl.ANY)


def hold_kernel(*refs):
    pass


def hold(values, *others):
    return pl.pallas_call(
        hold_kernel,
        in_specs=[ANY] * (1 + len(others)),
        out_specs=ANY,
        out_shape=jax.ShapeDtypeStruct(values.shape, values.dtype),
        input_output_aliases={0: 0},
        compiler_params=params(4),
        name="hold",
    )(values, *others)


def project_kernel(where, xa, xb, w, *refs):
    prompt_out, decode_out, rows_out, stats_out, rows = refs[-5:]
    core = where[1]
    own = xa.shape[0]
    rows[core] = xa[...]
    rows[1 - core] = xb[...]
    rows_out[...] = rows[:, 128:]
    both = jnp.concatenate([rows[0], rows[1]], axis=0)
    line = lax.broadcasted_iota(jnp.int32, (8, 256), 0)
    stats = jnp.zeros((8, 2 * own), jnp.float32)
    for part in range(3):
        made = jnp.dot(both, w[part], preferred_element_type=jnp.float32)
        made = made.astype(jnp.bfloat16)
        cols = pl.ds(part * 256, 256)
        for c in range(2):
            prompt_out[0, c, :, cols] = made[c * own : c * own + 64]
            prompt_out[1, c, :, cols] = made[c * own + 64 : c * own + 128]
            decode_out[c, :, cols] = made[c * own + 128 : (c + 1) * own]
        if part < 2:
            wide = made.astype(jnp.float32)
            stats = stats + lax.dot_general(
                jnp.where(line == part, 1.0, 0.0),
                wide * wide,
                (((1,), (1,)), ((), ())),
                precision=lax.Precision.HIGHEST,
                preferred_element_type=jnp.float32,
            )
    stats_out[0] = stats


def project(where, xa, xb, w, buffers, tokens=()):
    own, width = xa.shape
    shapes = [
        jax.ShapeDtypeStruct((2, 8, 64, 768), jnp.bfloat16),
        jax.ShapeDtypeStruct((8, own - 128, 768), jnp.bfloat16),
        jax.ShapeDtypeStruct((8, own - 128, width), jnp.bfloat16),
        jax.ShapeDtypeStruct((Z, 8, 2 * own), jnp.float32),
    ]
    grid_spec = pltpu.PrefetchScalarGridSpec(
        num_scalar_prefetch=1,
        grid=(1,),
        in_specs=[VMEM] * 3 + [ANY] * (len(buffers) + len(tokens)),
        out_specs=[
            pl.BlockSpec((2, 2, 64, 768), lambda i, s: (0, s[0], 0, 0)),
            pl.BlockSpec((2, own - 128, 768), lambda i, s: (s[0], 0, 0)),
            pl.BlockSpec((2, own - 128, width), lambda i, s: (s[0], 0, 0)),
            pl.BlockSpec((1, 8, 2 * own), lambda i, s: (s[0], 0, 0)),
        ],
        scratch_shapes=[pltpu.VMEM((2, own, width), jnp.bfloat16)],
    )
    return pl.pallas_call(
        project_kernel,
        grid_spec=grid_spec,
        out_shape=shapes,
        input_output_aliases={4 + i: i for i in range(len(buffers))},
        compiler_params=params(20),
        cost_estimate=pl.CostEstimate(
            flops=4 * own * width * 768, bytes_accessed=4 * 2**20, transcendentals=0
        ),
        name="project",
    )(where, xa, xb, w, *buffers, *tokens)


def swap_pairs(values):
    lane = lax.broadcasted_iota(jnp.int32, values.shape, 1)
    after = pltpu.roll(values, values.shape[1] - 1, 1)
    before = pltpu.roll(values, 1, 1)
    return jnp.where(lane % 2 == 0, after, before)


def attend_kernel(
    prompt, starts, q, k, v, g0, g1, g2, g3, scales, gain, cosine, sine, cached_at, *refs
):
    out, key_out = refs[-2:]
    cached = [
        jnp.concatenate([g[r, kind, 0] for g in (g0, g1, g2, g3) for r in range(2)], axis=0)
        for kind in range(2)
    ]
    width = 8 * 256
    scale = lax.rsqrt(jnp.transpose(scales[0]) / width + EPSILON)
    cos_t, sin_t = cosine[0], sine[0]

    def turn(raw, which):
        val = raw[0].astype(jnp.float32) * scale[:, which : which + 1] * gain[which : which + 1, :]
        return (val * cos_t + swap_pairs(val) * sin_t).astype(jnp.bfloat16)

    queries = turn(q, 0)
    keys = turn(k, 1)
    key_out[0] = keys
    dims = (((1,), (1,)), ((), ()))
    factor = HD ** (-0.5)
    rows = queries.shape[0]
    old = lax.dot_general(queries, cached[0], dims, preferred_element_type=jnp.float32) * factor
    new = lax.dot_general(queries, keys, dims, preferred_element_type=jnp.float32) * factor
    live_old = cached_at[...] < starts[prompt]
    live_new = lax.broadcasted_iota(jnp.int32, (rows, rows), 1) <= lax.broadcasted_iota(
        jnp.int32, (rows, rows), 0
    )
    old = jnp.where(live_old, old, MASKED_SCORE)
    new = jnp.where(live_new, new, MASKED_SCORE)
    top = jnp.maximum(
        jnp.max(old, axis=1, keepdims=True), jnp.max(new, axis=1, keepdims=True)
    )
    old = jnp.exp(old - top)
    new = jnp.exp(new - top)
    total = jnp.sum(old, axis=1, keepdims=True) + jnp.sum(new, axis=1, keepdims=True)
    mixed = jnp.dot(old.astype(jnp.bfloat16), cached[1], preferred_element_type=jnp.float32)
    mixed = mixed + jnp.dot(new.astype(jnp.bfloat16), v[0], preferred_element_type=jnp.float32)
    out[0] = (mixed / total).astype(jnp.bfloat16)


def attend(prompt, starts, qkv, cached, scales, gain, cosine, sine, cached_at, buffers, tokens):
    group = qkv.shape[1]
    part = cached[0].shape[3]
    ctx = 8 * part
    head = lambda off: pl.BlockSpec((1, group, HD), lambda h, s: (prompt, 0, off + h))
    grid_spec = pltpu.PrefetchScalarGridSpec(
        num_scalar_prefetch=1,
        grid=(2,),
        in_specs=[
            head(0),
            head(2),
            head(4),
            *[pl.BlockSpec((2, 2, 1, part, HD), lambda h, s: (0, 0, prompt, 0, h))] * Z,
            pl.BlockSpec((1, 8, group), lambda h, s: (prompt, 0, 0)),
            pl.BlockSpec((2, HD), lambda h, s: (0, h)),
            pl.BlockSpec((1, group, HD), lambda h, s: (prompt, 0, 0)),
            pl.BlockSpec((1, group, HD), lambda h, s: (prompt, 0, 0)),
            pl.BlockSpec((1, ctx), lambda h, s: (0, 0)),
        ]
        + [ANY] * (len(buffers) + len(tokens)),
        out_specs=[head(0), head(0)],
    )
    made = jax.ShapeDtypeStruct((2, group, 2 * HD), jnp.bfloat16)
    return pl.pallas_call(
        functools.partial(attend_kernel, prompt),
        grid_spec=grid_spec,
        out_shape=[made, made],
        input_output_aliases={13 + i: i for i in range(len(buffers))},
        compiler_params=params(16),
        cost_estimate=pl.CostEstimate(
            flops=8 * group * (group + ctx) * HD,
            bytes_accessed=6 * 2**20,
            transcendentals=2 * group * (group + ctx),
        ),
        name="attend",
    )(starts, qkv, qkv, qkv, *cached, scales, gain, cosine, sine, cached_at, *buffers, *tokens)


def decode_kernel(lengths, q, gains, cosine, sine, *refs):
    caches = refs[:4]
    mixed, marks, queries = refs[4:]
    step = pl.program_id(0)
    heads = q.shape[1] // HD
    width = q.shape[1]
    ctx = caches[0].shape[2]
    count = 8

    @pl.when(step == 0)
    def _():
        val = q[...].astype(jnp.float32)
        val = val * lax.rsqrt(jnp.mean(val * val, axis=1, keepdims=True) + EPSILON)
        val = val * gains[0:1, :]
        cos_t = jnp.concatenate([cosine[...]] * heads, axis=1)
        sin_t = jnp.concatenate([sine[...]] * heads, axis=1)
        val = val * cos_t + swap_pairs(val) * sin_t
        queries[...] = val.astype(jnp.bfloat16).astype(jnp.float32)

    first = lengths[lengths.shape[0] - 1]
    shape = (heads, width)
    own_head = lax.broadcasted_iota(jnp.int32, shape, 1) // HD == lax.broadcasted_iota(
        jnp.int32, shape, 0
    )
    rows, limits = [], []
    for j in range(count):
        slot = step * count + j
        row = jnp.broadcast_to(queries[pl.ds(slot, 1), :], shape)
        rows.append(jnp.where(own_head, row, 0.0).astype(jnp.bfloat16))
        limits.append(jnp.broadcast_to(lengths[slot] - first, (heads, 1)))
    keys = jnp.concatenate([cache[0, j] for cache in caches for j in range(2)], axis=0)
    values = jnp.concatenate([cache[1, j] for cache in caches for j in range(2)], axis=0)
    scores = lax.dot_general(
        jnp.concatenate(rows, axis=0),
        keys,
        (((1,), (1,)), ((), ())),
        preferred_element_type=jnp.float32,
    ) * HD ** (-0.5)
    size = (count * heads, count * ctx)
    line = lax.broadcasted_iota(jnp.int32, size, 0) // heads
    at = lax.broadcasted_iota(jnp.int32, size, 1) - line * ctx
    live = (at >= 0) & (at < ctx) & (at < jnp.concatenate(limits, axis=0))
    scores = jnp.where(live, scores, MASKED_SCORE)
    top = jnp.max(scores, axis=1, keepdims=True)
    weights = jnp.where(live, jnp.exp(scores - top), 0.0)
    total = jnp.sum(weights, axis=1, keepdims=True)
    marks[0, :, 0:1] = top
    marks[0, :, 1:2] = total
    part = jnp.dot(weights.astype(jnp.bfloat16), values, preferred_element_type=jnp.float32)
    for j in range(count):
        mixed[j : j + 1, :] = jnp.sum(
            jnp.where(own_head, part[j * heads : (j + 1) * heads], 0.0), axis=0, keepdims=True
        )


def decode(lengths, q, gains, cosine, sine, cache, skip):
    slots, width = q.shape
    ctx = cache.shape[2]
    heads = width // HD
    steps = slots // 8
    whole = lambda shape: pl.BlockSpec(shape, lambda i, s: (0, 0))
    pair = lambda j: pl.BlockSpec(
        (2, 2, ctx, width), lambda i, s: (0, i * 4 + j + skip // 2, 0, 0)
    )
    grid_spec = pltpu.PrefetchScalarGridSpec(
        num_scalar_prefetch=1,
        grid=(steps,),
        in_specs=[
            whole(q.shape),
            whole(gains.shape),
            whole(cosine.shape),
            whole(sine.shape),
        ]
        + [pair(j) for j in range(4)],
        out_specs=[
            pl.BlockSpec((8, width), lambda i, s: (i, 0)),
            pl.BlockSpec((1, 8 * heads, 2), lambda i, s: (i, 0, 0)),
        ],
        scratch_shapes=[pltpu.VMEM(q.shape, jnp.float32)],
    )
    mixed, marks = pl.pallas_call(
        decode_kernel,
        grid_spec=grid_spec,
        out_shape=[
            jax.ShapeDtypeStruct((slots, width), jnp.float32),
            jax.ShapeDtypeStruct((steps, 8 * heads, 2), jnp.float32),
        ],
        compiler_params=params(52),
        cost_estimate=pl.CostEstimate(
            flops=4 * slots * 128 * ctx * width, bytes_accessed=13 * 2**20, transcendentals=0
        ),
        name="decode",
    )(lengths, q, gains, cosine, sine, cache, cache, cache, cache)
    marks = marks.reshape(slots, heads, 2)
    return mixed, marks[..., 0], marks[..., 1]


def assemble_kernel(core, own, other, out, sems):
    made = []
    for j in range(4):
        for k, part in enumerate((own, other)):
            col = pl.multiple_of(j * 512 + (core[0] ^ k) * 256, 256)
            made.append(
                pltpu.make_async_copy(
                    part.at[j], out.at[:, pl.ds(col, 256)], sems.at[2 * j + k]
                )
            )
    for copy in made:
        copy.start()
    for copy in made:
        copy.wait()


def assemble(core, own, other):
    rows = own.shape[1]
    return pl.pallas_call(
        assemble_kernel,
        in_specs=[SMEM, ANY, ANY],
        out_specs=ANY,
        out_shape=jax.ShapeDtypeStruct((rows, 8 * 256), jnp.bfloat16),
        scratch_shapes=[pltpu.SemaphoreType.DMA((8,))],
        compiler_params=params(4),
        cost_estimate=pl.CostEstimate(flops=0, bytes_accessed=17 * 2**20, transcendentals=0),
        name="assemble",
    )(core, own, other)


def mix_kernel(where, *refs):
    lines = refs[:8]
    att, w, dec, dec_x, gain, out, xs, sems = refs[8:]
    step = pl.program_id(0)
    core = where[Z]
    copies = [
        pltpu.make_async_copy(lines[i], xs.at[where[i // 2], core ^ (i % 2)], sems.at[i])
        for i in range(8)
    ]

    @pl.when(step == 0)
    def _():
        for copy in copies:
            copy.start()

    sides = []
    for c in range(2):
        for p in range(2):
            sides.append(
                jnp.concatenate([att[k, p, c * 64 : (c + 1) * 64] for k in range(8)], axis=1)
            )
        sides.append(dec[c])
    rows = jnp.concatenate(sides, axis=0)
    total = jnp.dot(rows, w[...], preferred_element_type=jnp.float32)

    @pl.when(step == 0)
    def _():
        for copy in copies:
            copy.wait()

    inv = lax.rsqrt(jnp.mean(total * total, axis=1, keepdims=True) + EPSILON)
    total = total * inv * gain[2:3, :]
    per = 128 + BLOCK_PAD
    for c in range(2):
        base = c * per
        out[c, :128] = (
            xs[step, c, :128].astype(jnp.float32) + total[base : base + 128]
        ).astype(jnp.bfloat16)
        out[c, 128:] = (
            dec_x[c].astype(jnp.float32) + total[base + 128 : base + per]
        ).astype(jnp.bfloat16)


def mix(where, lines, att, w, dec, dec_x, gains):
    width = w.shape[1]
    return pl.pallas_call(
        mix_kernel,
        grid=(Z,),
        in_specs=[SMEM]
        + [ANY] * 8
        + [
            pl.BlockSpec((8, 2, 128, 256), lambda i: (0, 0, i, 0)),
            VMEM,
            pl.BlockSpec((2, BLOCK_PAD, width), lambda i: (i, 0, 0)),
            pl.BlockSpec((2, BLOCK_PAD, width), lambda i: (i, 0, 0)),
            pl.BlockSpec(gains.shape, lambda i: (0, 0)),
        ],
        out_specs=pl.BlockSpec((2, 128 + BLOCK_PAD, width), lambda i: (i, 0, 0)),
        out_shape=jax.ShapeDtypeStruct((8, 128 + BLOCK_PAD, width), jnp.bfloat16),
        scratch_shapes=[
            pltpu.VMEM((Z, 2) + lines[0].shape, jnp.bfloat16),
            pltpu.SemaphoreType.DMA((8,)),
        ],
        compiler_params=params(18),
        cost_estimate=pl.CostEstimate(
            flops=2 * 8 * 144 * width * width, bytes_accessed=22 * 2**20, transcendentals=0
        ),
        name="mix",
    )(where, *lines, att, w, dec, dec_x, gains)


def deliver_kernel(where, a, b, c, d, prompt_out, decode_out):
    for k, part in enumerate((a, b, c, d)):
        for r in range(2):
            cols = pl.ds(pl.multiple_of(where[2 * k + r] * 256, 256), 256)
            for kind in range(2):
                block = part[r, kind]
                prompt_out[kind, :, cols] = block[:128]
                decode_out[kind, :, cols] = block[128:]


def deliver(where, came, width):
    own = came[0].shape[2]
    return pl.pallas_call(
        deliver_kernel,
        in_specs=[SMEM] + [VMEM] * 4,
        out_specs=[VMEM, VMEM],
        out_shape=[
            jax.ShapeDtypeStruct((2, 128, width), jnp.bfloat16),
            jax.ShapeDtypeStruct((2, own - 128, width), jnp.bfloat16),
        ],
        compiler_params=params(8),
        cost_estimate=pl.CostEstimate(flops=0, bytes_accessed=2**22, transcendentals=0),
        name="deliver",
    )(where, *came)


def forward_kernel(where, hidden, wgu, wd, *refs):
    mine, other, acc = refs[-3:]
    per = hidden.shape[1]
    rows = hidden[pl.ds(where[0] * 2, 2)].reshape(2 * per, hidden.shape[2])
    half = wd.shape[0] // 2
    total = None
    for i in range(2):
        cols = pl.ds(i * half, half)
        gate = jnp.dot(rows, wgu[0, :, cols], preferred_element_type=jnp.float32)
        up = jnp.dot(rows, wgu[1, :, cols], preferred_element_type=jnp.float32)
        act = (gate / (1.0 + jnp.exp(-gate)) * up).astype(jnp.bfloat16)
        part = jnp.dot(act, wd[cols], preferred_element_type=jnp.float32)
        total = part if total is None else total + part
    acc[...] = total.reshape(acc.shape)
    core = where[1]
    mine[...] = acc[core, : mine.shape[0]].astype(jnp.bfloat16)
    other[...] = acc[1 - core, : mine.shape[0]].astype(jnp.bfloat16)


def forward(where, hidden, wgu, wd, rows, tokens):
    per, width = hidden.shape[1:]
    made = jax.ShapeDtypeStruct((rows, width), jnp.bfloat16)
    return pl.pallas_call(
        forward_kernel,
        in_specs=[SMEM, VMEM, VMEM, VMEM] + [ANY] * len(tokens),
        out_specs=[VMEM, VMEM],
        out_shape=[made, made],
        scratch_shapes=[pltpu.VMEM((2, per, width), jnp.float32)],
        compiler_params=params(12),
        cost_estimate=pl.CostEstimate(
            flops=12 * per * width * wd.shape[0], bytes_accessed=4 * 2**20, transcendentals=0
        ),
        name="forward",
    )(where, hidden, wgu, wd, *tokens)


def tables(positions):
    lanes = jnp.arange(HD, dtype=jnp.int32)
    freq_index = (lanes // 2).astype(jnp.float32)
    inv_freq = jnp.power(ROPE_BASE, -2.0 * freq_index / HD)
    angles = positions.astype(jnp.float32)[..., None] * inv_freq
    sign = jnp.where(lanes % 2 == 0, -1.0, 1.0)
    return jnp.cos(angles), jnp.sin(angles) * sign


def turn_kernel(where, a, b, up, down, up_out, down_out):
    chip = where[0]
    one, two = a[...].astype(jnp.float32), b[...].astype(jnp.float32)
    up_out[...] = (jnp.where(chip == 1, one, two) + up[...]).astype(jnp.bfloat16)
    down_out[...] = (jnp.where(chip == 2, one, two) + down[...]).astype(jnp.bfloat16)


def turn_sums(where, a, b, up, down):
    made = jax.ShapeDtypeStruct(a.shape, a.dtype)
    return pl.pallas_call(
        turn_kernel,
        in_specs=[SMEM] + [VMEM] * 4,
        out_specs=[VMEM, VMEM],
        out_shape=[made, made],
        compiler_params=params(10),
        cost_estimate=pl.CostEstimate(flops=0, bytes_accessed=2**22, transcendentals=0),
        name="turn_sums",
    )(where, a, b, up, down)


def narrow_sum(*terms):
    total = terms[0].astype(jnp.float32)
    for term in terms[1:]:
        total = total + term.astype(jnp.float32)
    return total.astype(jnp.bfloat16)


def after(values, *others):
    return lax.optimization_barrier((values,) + others)[0]


def local_heads(
    prompt_states,
    decode_states,
    cache,
    prompt_starts,
    decode_lengths,
    decode_slots,
    w_qkv,
    w_out,
    w_gate_up,
    w_down,
    gains,
):
    place = lax.axis_index("tensor")
    chip, core = place // 2, place % 2
    data_pos = lax.axis_index("dp")
    pre_dev, part_rows, width = prompt_states.shape
    dec_part = decode_states.shape[0]
    group = part_rows * 8
    dec_dev = dec_part * 8
    ctx_part = cache.shape[2]
    heads = width // HD
    own_rows = pre_dev * part_rows + dec_part
    states = jnp.concatenate(
        [prompt_states.reshape(pre_dev * part_rows, width), decode_states], axis=0
    )
    starts = lax.dynamic_slice_in_dim(prompt_starts, data_pos * pre_dev, pre_dev)
    slot_ids = data_pos * dec_dev + jnp.arange(dec_dev, dtype=jnp.int32)
    matches = decode_slots[None, :] == slot_ids[:, None]
    slot_length = jnp.sum(jnp.where(matches, decode_lengths[None, :], 0), axis=1)
    prompt_pos = starts[:, None] + jnp.arange(group, dtype=jnp.int32)[None, :]
    cos_p, sin_p = tables(prompt_pos)
    cos_d, sin_d = tables(slot_length)
    my_gains = lax.dynamic_slice_in_dim(gains[:2], place * 256, 256, 1)

    chips_at = (chip - jnp.arange(Z, dtype=jnp.int32)) % Z
    blocks_at = jnp.stack([chips_at * 2 + core, chips_at * 2 + 1 - core], axis=1).astype(jnp.int32)
    low, end = chip < 2, (chip == 0) | (chip == Z - 1)

    lines = []

    def add_block(line, source, buffers, *tokens):
        at = jnp.stack([source, core]).astype(jnp.int32)
        other = send(line, CORE)
        lines.extend([line, other])
        return project(at, line, other, w_qkv, buffers, tokens)

    rise1, fall1 = send(states, UP[0]), send(states, DOWN[0])
    prompt_cache = cache[:, :pre_dev]
    prompt_cache = jnp.stack(
        [
            jnp.stack(
                [prompt_cache[..., (2 * z + c) * 256 : (2 * z + c + 1) * 256] for c in range(2)]
            )
            for z in range(Z)
        ]
    )
    cache_pair = swap_cores(prompt_cache, core)
    buffers = add_block(states, chip, (), cache_pair)
    rise2, fall2 = send(rise1, UP[1]), send(fall1, DOWN[1])
    line = jnp.where(chip % 2 == 0, fall1, rise1)
    buffers = add_block(line, chip ^ 1, buffers)
    rise2, fall2, *buffers = lax.optimization_barrier((rise2, fall2, *buffers))
    rise3, fall3 = send(rise2, UP[2]), send(fall2, DOWN[2])
    line = jnp.where(low, jnp.where(end, fall2, fall1), jnp.where(end, rise2, rise1))
    buffers = add_block(line, jnp.where(low, 2, 1), buffers)
    rise3, fall3, *buffers = lax.optimization_barrier((rise3, fall3, *buffers))
    line = jnp.where(low, jnp.where(end, fall3, fall2), jnp.where(end, rise3, rise2))
    buffers = add_block(line, jnp.where(low, 3, 0), buffers)
    prompt_raw, decode_raw, dec_x, stats = buffers
    prompt_raw = prompt_raw.reshape(pre_dev, group, 768)
    decode_raw = decode_raw.reshape(dec_dev, 768)

    cached_at = (
        blocks_at.reshape(8, 1) * ctx_part + jnp.arange(ctx_part, dtype=jnp.int32)[None, :]
    ).reshape(1, 8 * ctx_part)

    stats = small_sum(stats).reshape(Z, 8, 2, own_rows)
    prompt_stats = stats[..., : own_rows - dec_part].reshape(Z, 8, 2, pre_dev, part_rows)
    prompt_stats = jnp.transpose(prompt_stats, (3, 1, 0, 2, 4)).reshape(pre_dev, 8, group)
    dec_stats = jnp.transpose(stats[..., own_rows - dec_part :], (0, 2, 3, 1)).reshape(dec_dev, 8)
    dec_scales = lax.rsqrt(dec_stats / width + EPSILON)
    def turn(raw, scale, gain):
        val = raw.astype(jnp.float32) * scale * gain
        even = jnp.arange(val.shape[1]) % 2 == 0
        swapped = jnp.where(even, jnp.roll(val, -1, axis=1), jnp.roll(val, 1, axis=1))
        cos_t = jnp.concatenate([cos_d] * 2, axis=1)
        sin_t = jnp.concatenate([sin_d] * 2, axis=1)
        return (val * cos_t + swapped * sin_t).astype(jnp.bfloat16).reshape(-1, 2, HD)

    query_mine = turn(decode_raw[:, :256], dec_scales[:, :1], my_gains[0])
    key_mine = turn(decode_raw[:, 256:512], dec_scales[:, 1:2], my_gains[1])
    value_mine = decode_raw[:, 512:].reshape(dec_dev, 2, HD)
    query_all = small_gather(decode_raw[:, :256], chip, core)
    query_all = jnp.swapaxes(query_all, 0, 1).reshape(dec_dev, width)

    share = width // 4
    w_share = lax.dynamic_slice_in_dim(w_out, data_pos * share, share, 1)
    w_share = w_share.reshape(1, w_out.shape[0], 2, share // 2)
    w_pair = swap_cores(jnp.transpose(w_share, (0, 2, 1, 3)), core)[0]
    w_pair = jnp.where(core == 0, w_pair, w_pair[::-1])
    lanes = [[2 * z + c for z in range(Z)] for c in range(2)]
    w_line = lax.all_gather(w_pair, "tensor", axis=0, axis_index_groups=lanes)
    w_line = hold(w_line, query_all)
    w_own = lax.all_gather(w_line.reshape(width, share // 2), "dp", axis=0)
    w_full = assemble(core[None].astype(jnp.int32), w_own, send(w_own, CORE))

    got = spread_chips(hold(cache_pair, query_all), chip)
    scale_factor = HD ** (-0.5)
    lengths = jnp.concatenate([slot_length, (place * ctx_part)[None]]).astype(jnp.int32)
    mixed, tops, sums = decode(lengths, query_all, gains, cos_d, sin_d, cache, pre_dev)
    parts = jnp.concatenate(
        [
            jnp.transpose(mixed.reshape(dec_dev, 8, 256), (1, 0, 2)),
            jnp.transpose(tops.reshape(dec_dev, 8, 2), (1, 0, 2)),
            jnp.transpose(sums.reshape(dec_dev, 8, 2), (1, 0, 2)),
        ],
        axis=-1,
    )
    parts = swap_cores(parts.reshape(Z, 2, dec_dev, 260), core)
    arrived = spread_chips(parts, chip)
    made = ()
    for prompt, tokens in enumerate(((parts,), arrived)):
        made = attend(
            prompt,
            starts,
            prompt_raw,
            got,
            prompt_stats,
            my_gains,
            cos_p,
            sin_p,
            cached_at,
            made,
            tokens,
        )
    attended, key_new = made
    arrived = jnp.stack(arrived).reshape(8, dec_dev, 260)
    got_mixed = arrived[..., :256].reshape(8, dec_dev, 2, HD)
    got_tops, got_sums = arrived[..., 256:258], arrived[..., 258:]
    own_score = (
        jnp.sum(query_mine.astype(jnp.float32) * key_mine.astype(jnp.float32), axis=-1)
        * scale_factor
    )
    highest = jnp.maximum(jnp.max(got_tops, axis=0), own_score)
    factors = jnp.exp(got_tops - highest[None])
    own_weight = jnp.exp(own_score - highest)
    total = jnp.sum(got_sums * factors, axis=0) + own_weight
    summed = jnp.sum(got_mixed * factors[..., None], axis=0)
    summed = summed + own_weight.astype(jnp.bfloat16).astype(jnp.float32)[
        ..., None
    ] * value_mine.astype(jnp.float32)
    dec_attended = (summed / total[..., None]).reshape(dec_dev, 256).astype(jnp.bfloat16)
    wanted = lax.dynamic_slice_in_dim(decode_slots, data_pos * dec_dev, dec_dev)
    by_request = jnp.take(
        data_gather(dec_attended, data_pos).reshape(4 * dec_dev, 256), wanted, axis=0
    )
    pad = lambda v: jnp.pad(
        v.reshape(8, dec_part, width), ((0, 0), (0, BLOCK_PAD - dec_part), (0, 0))
    )
    dec_rows = small_gather(by_request, chip, core)
    dec_rows = pad(jnp.swapaxes(dec_rows, 0, 1).reshape(dec_dev, width))
    dec_x = after(dec_x.reshape(dec_dev, width), attended)
    dec_x = data_gather(dec_x, data_pos)
    dec_x = pad(jnp.take(dec_x.reshape(4 * dec_dev, width), wanted, axis=0))

    fresh = jnp.stack([key_new, prompt_raw[:, :, 512:]])
    fresh = fresh.reshape(2, pre_dev, 8, part_rows, 256)
    fresh = jnp.transpose(fresh, (2, 0, 1, 3, 4)).reshape(8, 2, pre_dev * part_rows, 256)
    fresh_dec = jnp.stack([key_mine.reshape(dec_dev, 256), decode_raw[:, 512:]])
    fresh_dec = jnp.transpose(fresh_dec.reshape(2, 8, dec_part, 256), (1, 0, 2, 3))
    fresh = jnp.concatenate([fresh, fresh_dec], axis=2)
    fresh_pair = swap_cores(fresh.reshape(Z, 2, 2, own_rows, 256), core)

    att = lax.all_gather(attended, "tensor", axis=0)
    fresh_pair = after(fresh_pair, att)
    kv_came = spread_chips(fresh_pair, chip)
    where = jnp.stack(
        [chip, chip ^ 1, jnp.where(low, 2, 1), jnp.where(low, 3, 0), core]
    ).astype(jnp.int32)
    hidden = mix(where, lines, att, w_full, dec_rows, dec_x, gains)

    orders = jnp.array([[3, 2, 1, 0], [3, 2, 0, 1], [0, 1, 3, 2], [0, 1, 2, 3]], jnp.int32)
    order = lax.dynamic_index_in_dim(orders, chip, 0, keepdims=False)
    sums = []
    for k in range(Z):
        at = jnp.stack([order[k], core]).astype(jnp.int32)
        tokens = [kv_came, sums, (), ()][k]
        mine, other = forward(at, hidden, w_gate_up, w_down, own_rows, tokens)
        sums.append(narrow_sum(mine, send(other, CORE)))
    came = after(send(sums[0], ENDS), mine)
    is_end = (chip == 0) | (chip == 3)
    load = narrow_sum(jnp.where(is_end, sums[1], sums[0]), came)
    up, down = send(load, RISE[0]), send(load, FALL[0])
    up, down = turn_sums(chip[None].astype(jnp.int32), sums[1], sums[2], up, down)
    up, down = send(up, RISE[1]), send(down, FALL[1])
    ffn_sum = sums[3].astype(jnp.float32) + up.astype(jnp.float32) + down.astype(jnp.float32)
    hidden_own = lax.dynamic_index_in_dim(hidden, place, 0, keepdims=False)[:own_rows]
    output = (hidden_own.astype(jnp.float32) + rms_scale(ffn_sum, gains[3])).astype(jnp.bfloat16)
    prompt_out = output[: own_rows - dec_part].reshape(pre_dev, part_rows, width)
    decode_out = output[own_rows - dec_part :]

    new_prompt_kv, new_decode_kv = deliver(blocks_at.reshape(8), kv_came, width)
    new_prompt_kv = new_prompt_kv.reshape(2, pre_dev, part_rows, width)
    return (prompt_out, decode_out, new_prompt_kv, new_decode_kv)


def fits_heads(mesh):
    return mesh.shape["tensor"] == 2 * Z and mesh.shape["dp"] == 4


def solution(mesh):
    in_specs = (
        P("dp", "tensor", None),
        P(("dp", "tensor"), None),
        P(None, "dp", "tensor", None),
        P(),
        P(),
        P(),
        P(None, None, "tensor"),
        P("tensor", None),
        P(None, None, "tensor"),
        P("tensor", None),
        P(),
    )
    out_specs = (
        P("dp", "tensor", None),
        P(("dp", "tensor"), None),
        P(None, "dp", "tensor", None),
        P(None, ("dp", "tensor"), None),
    )
    body = local_heads if fits_heads(mesh) else local
    return jax.shard_map(body, mesh=mesh, in_specs=in_specs, out_specs=out_specs, check_vma=False)
```

```python
import functools

import jax
import jax.numpy as jnp
from jax import lax
from jax.experimental import pallas as pl
from jax.experimental.pallas import tpu as pltpu
from jax.sharding import PartitionSpec as P

HD = 128


EPSILON = 1e-06
ROPE_BASE = 500000.0
MASKED_SCORE = -1e30


def rms_scale(values, gain_vec):
    return (
        values * lax.rsqrt(jnp.mean(values * values, axis=-1, keepdims=True) + EPSILON) * gain_vec
    )


def rotate(values, positions):
    full_shape = values.shape
    paired = values.reshape(full_shape[:-1] + (full_shape[-1] // HD, HD // 2, 2))
    freq_index = jnp.arange(HD // 2, dtype=jnp.float32)
    inv_freq = jnp.power(ROPE_BASE, -2.0 * freq_index / HD)
    angles = positions.astype(jnp.float32)[..., None, None] * inv_freq
    cosine = jnp.cos(angles)
    sine_values = jnp.sin(angles)
    even_part = paired[..., 0]
    odd_part = paired[..., 1]
    turned = jnp.stack(
        [even_part * cosine - odd_part * sine_values, even_part * sine_values + odd_part * cosine],
        axis=-1,
    )
    return turned.reshape(full_shape)


def split_rows(stacked, tensors, pre_dev, part_rows):
    tail_shape = stacked.shape[1:]
    per_device = stacked.shape[0] // tensors
    device_grid = stacked.reshape((tensors, per_device) + tail_shape)
    prompt_part = device_grid[:, : pre_dev * part_rows].reshape(
        (tensors, pre_dev, part_rows) + tail_shape
    )
    prompt_part = jnp.swapaxes(prompt_part, 0, 1).reshape(
        (pre_dev, tensors * part_rows) + tail_shape
    )
    decode_part = device_grid[:, pre_dev * part_rows :].reshape((-1,) + tail_shape)
    return (prompt_part, decode_part)


def join_rows(prompt_part, decode_part, tensors):
    pre_dev = prompt_part.shape[0]
    part_rows = prompt_part.shape[1] // tensors
    tail_shape = prompt_part.shape[2:]
    leading = jnp.swapaxes(prompt_part.reshape((pre_dev, tensors, part_rows) + tail_shape), 0, 1)
    leading = leading.reshape((tensors, pre_dev * part_rows) + tail_shape)
    trailing = decode_part.reshape((tensors, -1) + tail_shape)
    return jnp.concatenate([leading, trailing], axis=1).reshape((-1,) + tail_shape)


def spread(local_rows, weights):
    return jnp.einsum(
        "rd,kdc->rkc",
        lax.all_gather(local_rows, "tensor", axis=0, tiled=True),
        weights,
        preferred_element_type=jnp.float32,
    )


def collect(operand, weights):
    return lax.psum_scatter(
        jnp.dot(operand, weights, preferred_element_type=jnp.float32).astype(jnp.bfloat16),
        "tensor",
        scatter_dimension=0,
        tiled=True,
    ).astype(jnp.float32)


def local(
    prompt_states,
    decode_states,
    cache,
    prompt_starts,
    decode_lengths,
    decode_slots,
    w_qkv,
    w_out,
    w_gate_up,
    w_down,
    gains,
):
    tensors = lax.axis_size("tensor")
    tensor_pos = lax.axis_index("tensor")
    data_pos = lax.axis_index("dp")
    pre_dev, part_rows, model_width = prompt_states.shape
    dec_part = decode_states.shape[0]
    group_len = part_rows * tensors
    dec_dev = dec_part * tensors
    ctx_part = cache.shape[2]
    head_count = model_width // HD
    prompt_own = pre_dev * part_rows
    own_rows = prompt_own + dec_part
    states = jnp.concatenate(
        [prompt_states.reshape(prompt_own, model_width), decode_states], axis=0
    )
    starts = lax.dynamic_slice_in_dim(prompt_starts, data_pos * pre_dev, pre_dev)
    slot_ids = data_pos * dec_dev + jnp.arange(dec_dev, dtype=jnp.int32)
    matches = decode_slots[None, :] == slot_ids[:, None]
    slot_length = jnp.sum(jnp.where(matches, decode_lengths[None, :], 0), axis=1)
    offsets = jnp.arange(group_len, dtype=jnp.int32)
    prompt_pos = starts[:, None] + offsets[None, :]
    own_prompt_pos = lax.dynamic_slice_in_dim(
        prompt_pos, tensor_pos * part_rows, part_rows, 1
    ).reshape(prompt_own)
    own_decode_pos = lax.dynamic_slice_in_dim(slot_length, tensor_pos * dec_part, dec_part)
    own_pos = jnp.concatenate([own_prompt_pos, own_decode_pos], axis=0)
    projected = spread(states, w_qkv)
    query_raw = projected[:, 0].astype(jnp.bfloat16)
    key_raw = projected[:, 1].astype(jnp.bfloat16)
    value_raw = projected[:, 2].astype(jnp.bfloat16)
    query_all, key_all, value_all = (
        lax.all_gather(query_raw, "tensor", axis=1, tiled=True),
        lax.all_gather(key_raw, "tensor", axis=1, tiled=True),
        lax.all_gather(value_raw, "tensor", axis=1, tiled=True),
    )
    key_own = lax.dynamic_slice_in_dim(key_all, tensor_pos * own_rows, own_rows, 0)
    value_own = lax.dynamic_slice_in_dim(value_all, tensor_pos * own_rows, own_rows, 0)
    query_prompt, query_decode = split_rows(query_all, tensors, pre_dev, part_rows)
    query_prompt = rotate(rms_scale(query_prompt.astype(jnp.float32), gains[0]), prompt_pos).astype(
        jnp.bfloat16
    )
    query_decode = rotate(
        rms_scale(query_decode.astype(jnp.float32), gains[0]), slot_length
    ).astype(jnp.bfloat16)
    key_new = rotate(rms_scale(key_own.astype(jnp.float32), gains[1]), own_pos).astype(jnp.bfloat16)
    scale_factor = HD ** (-0.5)
    cache_pos = tensor_pos * ctx_part + jnp.arange(ctx_part, dtype=jnp.int32)
    prompt_q = query_prompt.reshape(pre_dev, group_len, head_count, HD)
    prompt_keys = cache[0, :pre_dev].reshape(pre_dev, ctx_part, head_count, HD)
    prompt_values = cache[1, :pre_dev].reshape(pre_dev, ctx_part, head_count, HD)
    fresh_keys = key_new[:prompt_own].reshape(pre_dev, part_rows, head_count, HD)
    fresh_values = value_own[:prompt_own].reshape(pre_dev, part_rows, head_count, HD)
    cached_scores = jnp.einsum(
        "aihe,ajhe->ahij", prompt_q, prompt_keys, preferred_element_type=jnp.float32
    )
    fresh_scores = jnp.einsum(
        "aihe,ajhe->ahij", prompt_q, fresh_keys, preferred_element_type=jnp.float32
    )
    prompt_scores = jnp.concatenate([cached_scores, fresh_scores], axis=-1) * scale_factor
    key_offsets = tensor_pos * part_rows + jnp.arange(part_rows, dtype=jnp.int32)
    live_cached = jnp.broadcast_to(
        (cache_pos[None, :] < starts[:, None])[:, None, None, :], (pre_dev, 1, group_len, ctx_part)
    )
    live_fresh = jnp.broadcast_to(
        (key_offsets[None, :] <= offsets[:, None])[None, None], (pre_dev, 1, group_len, part_rows)
    )
    prompt_live = jnp.concatenate([live_cached, live_fresh], axis=-1)
    prompt_masked = jnp.where(prompt_live, prompt_scores, MASKED_SCORE)
    prompt_top = jnp.max(prompt_masked, axis=-1)
    decode_q = query_decode.reshape(dec_dev, head_count, HD)
    decode_keys = cache[0, pre_dev:].reshape(dec_dev, ctx_part, head_count, HD)
    decode_values = cache[1, pre_dev:].reshape(dec_dev, ctx_part, head_count, HD)
    own_keys = key_new[prompt_own:].reshape(dec_part, head_count, HD)
    own_values = value_own[prompt_own:].reshape(dec_part, head_count, HD)
    decode_cached = jnp.einsum(
        "she,sjhe->shj", decode_q, decode_keys, preferred_element_type=jnp.float32
    )
    decode_fresh = jnp.einsum(
        "she,jhe->shj", decode_q, own_keys, preferred_element_type=jnp.float32
    )
    decode_scores = jnp.concatenate([decode_cached, decode_fresh], axis=-1) * scale_factor
    live_slots = (cache_pos[None, :] < slot_length[:, None])[:, None, :]
    own_ids = tensor_pos * dec_part + jnp.arange(dec_part, dtype=jnp.int32)
    live_owned = (jnp.arange(dec_dev, dtype=jnp.int32)[:, None] == own_ids[None, :])[:, None, :]
    decode_live = jnp.concatenate([live_slots, live_owned], axis=-1)
    decode_masked = jnp.where(decode_live, decode_scores, MASKED_SCORE)
    decode_top = jnp.max(decode_masked, axis=-1)
    prompt_weights = jnp.where(prompt_live, jnp.exp(prompt_masked - prompt_top[..., None]), 0.0)
    prompt_total = jnp.sum(prompt_weights, axis=-1)
    prompt_probs = prompt_weights.astype(jnp.bfloat16)
    prompt_mixed = jnp.einsum(
        "ahij,ajhe->aihe",
        prompt_probs[..., :ctx_part],
        prompt_values,
        preferred_element_type=jnp.float32,
    )
    prompt_mixed = prompt_mixed + jnp.einsum(
        "ahij,ajhe->aihe",
        prompt_probs[..., ctx_part:],
        fresh_values,
        preferred_element_type=jnp.float32,
    )
    decode_weights = jnp.where(decode_live, jnp.exp(decode_masked - decode_top[..., None]), 0.0)
    decode_total = jnp.sum(decode_weights, axis=-1)
    decode_probs = decode_weights.astype(jnp.bfloat16)
    decode_mixed = jnp.einsum(
        "shj,sjhe->she",
        decode_probs[..., :ctx_part],
        decode_values,
        preferred_element_type=jnp.float32,
    )
    decode_mixed = decode_mixed + jnp.einsum(
        "shj,jhe->she", decode_probs[..., ctx_part:], own_values, preferred_element_type=jnp.float32
    )
    totals = join_rows(jnp.swapaxes(prompt_total, 1, 2), decode_total, tensors)
    mixed = join_rows(
        prompt_mixed.reshape(pre_dev, group_len, model_width),
        decode_mixed.reshape(dec_dev, model_width),
        tensors,
    )
    tops = join_rows(jnp.swapaxes(prompt_top, 1, 2), decode_top, tensors)
    got_tops, got_totals, got_mixed = (
        lax.all_to_all(tops, "tensor", split_axis=0, concat_axis=0, tiled=True),
        lax.all_to_all(totals, "tensor", split_axis=0, concat_axis=0, tiled=True),
        lax.all_to_all(mixed, "tensor", split_axis=0, concat_axis=0, tiled=True),
    )
    got_tops = got_tops.reshape(tensors, own_rows, head_count)
    got_totals = got_totals.reshape(tensors, own_rows, head_count)
    got_mixed = got_mixed.reshape(tensors, own_rows, head_count, HD)
    highest = jnp.max(got_tops, axis=0)
    factors = jnp.exp(got_tops - highest[None])
    total_all = jnp.sum(got_totals * factors, axis=0)
    shares = lax.optimization_barrier((got_mixed * factors[..., None]).astype(jnp.bfloat16))
    mixed_all = jnp.sum(shares.astype(jnp.float32), axis=0)
    attended_own = (
        (mixed_all / total_all[..., None]).reshape(own_rows, model_width).astype(jnp.bfloat16)
    )
    my_columns = lax.all_to_all(attended_own, "tensor", split_axis=1, concat_axis=0, tiled=True)
    attn_sum = collect(my_columns, w_out)
    hidden = (states.astype(jnp.float32) + rms_scale(attn_sum, gains[2])).astype(jnp.bfloat16)
    gate_up = spread(hidden, w_gate_up)
    activated = (jax.nn.silu(gate_up[:, 0]) * gate_up[:, 1]).astype(jnp.bfloat16)
    ffn_sum = collect(activated, w_down)
    output = (hidden.astype(jnp.float32) + rms_scale(ffn_sum, gains[3])).astype(jnp.bfloat16)
    prompt_out = output[:prompt_own].reshape(pre_dev, part_rows, model_width)
    everyone = lax.all_gather(output[prompt_own:], ("dp", "tensor"), axis=0, tiled=True)
    wanted = lax.dynamic_slice_in_dim(
        decode_slots, (data_pos * tensors + tensor_pos) * dec_part, dec_part
    )
    decode_out = jnp.take(everyone, wanted, axis=0)
    new_prompt_kv = jnp.stack([key_new[:prompt_own], value_own[:prompt_own]]).reshape(
        2, pre_dev, part_rows, model_width
    )
    new_decode_kv = jnp.stack([key_new[prompt_own:], value_own[prompt_own:]])
    return (prompt_out, decode_out, new_prompt_kv, new_decode_kv)


Z = 4
BLOCK_PAD = 16


def z_pairs(targets):
    return [(z * 2 + c, t * 2 + c) for z in range(Z) for t in targets(z) for c in range(2)]


CORE = [(i, i ^ 1) for i in range(2 * Z)]
UP = [z_pairs(lambda z, k=k: [z + 1] if k <= z < Z - 1 else []) for k in range(Z - 1)]
DOWN = [z_pairs(lambda z, k=k: [z - 1] if 0 < z <= Z - 1 - k else []) for k in range(Z - 1)]
TURN = [z_pairs(lambda z, k=k: [(z + k) % Z]) for k in range(1, Z)]
ENDS = z_pairs(lambda z: {0: [1], 3: [2]}.get(z, []))
RISE = [z_pairs(lambda z: [z + 1] if z < 2 else []), z_pairs(lambda z: [z + 1] if z < 3 else [])]
FALL = [z_pairs(lambda z: [z - 1] if z > 1 else []), z_pairs(lambda z: [z - 1] if z > 0 else [])]


def send(values, pairs):
    return lax.ppermute(values, "tensor", pairs)


def small_gather(values, chip, core):
    pair = jnp.stack([values, send(values, CORE)])
    pair = jnp.where(core == 0, pair, pair[::-1])
    chips = jnp.stack([pair] + [send(pair, TURN[k]) for k in range(Z - 1)])
    order = (chip - jnp.arange(Z, dtype=jnp.int32)) % Z
    return jnp.take(chips, order, axis=0).reshape((2 * Z,) + values.shape)


def small_sum(values):
    total = values + send(values, CORE)
    parts = [send(total, TURN[k]) for k in range(Z - 1)]
    return total + parts[1] + (parts[0] + parts[2])


def exchange(blocks, chip, core):
    return spread_chips(swap_cores(blocks, core), chip)


def swap_cores(blocks, core):
    mine = lax.dynamic_index_in_dim(blocks, core, 1, keepdims=False)
    other = lax.dynamic_index_in_dim(blocks, 1 - core, 1, keepdims=False)
    return jnp.stack([mine, send(other, CORE)], axis=1)


def spread_chips(both, chip):
    got = [lax.dynamic_index_in_dim(both, chip, 0, keepdims=False)]
    for k in range(1, Z):
        part = lax.dynamic_index_in_dim(both, (chip + k) % Z, 0, keepdims=False)
        got.append(send(part, TURN[k - 1]))
    return got


def data_gather(values, data_pos):
    first = jnp.stack([values, lax.ppermute(values, "dp", [(i, i ^ 1) for i in range(4)])])
    second = lax.ppermute(first, "dp", [(i, i ^ 2) for i in range(4)])
    both = jnp.concatenate([first, second])
    return jnp.take(both, jnp.arange(4, dtype=jnp.int32) ^ data_pos, axis=0)


def params(limit):
    return pltpu.CompilerParams(vmem_limit_bytes=limit * 2**20)


VMEM = pl.BlockSpec(memory_space=pltpu.VMEM)
SMEM = pl.BlockSpec(memory_space=pltpu.SMEM)
ANY = pl.BlockSpec(memory_space=pl.ANY)


def hold_kernel(*refs):
    pass


def hold(values, *others):
    return pl.pallas_call(
        hold_kernel,
        in_specs=[ANY] * (1 + len(others)),
        out_specs=ANY,
        out_shape=jax.ShapeDtypeStruct(values.shape, values.dtype),
        input_output_aliases={0: 0},
        compiler_params=params(4),
        name="hold",
    )(values, *others)


def project_kernel(where, xa, xb, w, *refs):
    prompt_out, decode_out, rows_out, stats_out, rows = refs[-5:]
    core = where[1]
    own = xa.shape[0]
    rows[core] = xa[...]
    rows[1 - core] = xb[...]
    rows_out[...] = rows[:, 128:]
    both = jnp.concatenate([rows[0], rows[1]], axis=0)
    line = lax.broadcasted_iota(jnp.int32, (8, 256), 0)
    stats = jnp.zeros((8, 2 * own), jnp.float32)
    for part in range(3):
        made = jnp.dot(both, w[part], preferred_element_type=jnp.float32)
        made = made.astype(jnp.bfloat16)
        cols = pl.ds(part * 256, 256)
        for c in range(2):
            prompt_out[0, c, :, cols] = made[c * own : c * own + 64]
            prompt_out[1, c, :, cols] = made[c * own + 64 : c * own + 128]
            decode_out[c, :, cols] = made[c * own + 128 : (c + 1) * own]
        if part < 2:
            wide = made.astype(jnp.float32)
            stats = stats + lax.dot_general(
                jnp.where(line == part, 1.0, 0.0),
                wide * wide,
                (((1,), (1,)), ((), ())),
                precision=lax.Precision.HIGHEST,
                preferred_element_type=jnp.float32,
            )
    stats_out[0] = stats


def project(where, xa, xb, w, buffers, tokens=()):
    own, width = xa.shape
    shapes = [
        jax.ShapeDtypeStruct((2, 8, 64, 768), jnp.bfloat16),
        jax.ShapeDtypeStruct((8, own - 128, 768), jnp.bfloat16),
        jax.ShapeDtypeStruct((8, own - 128, width), jnp.bfloat16),
        jax.ShapeDtypeStruct((Z, 8, 2 * own), jnp.float32),
    ]
    grid_spec = pltpu.PrefetchScalarGridSpec(
        num_scalar_prefetch=1,
        grid=(1,),
        in_specs=[VMEM] * 3 + [ANY] * (len(buffers) + len(tokens)),
        out_specs=[
            pl.BlockSpec((2, 2, 64, 768), lambda i, s: (0, s[0], 0, 0)),
            pl.BlockSpec((2, own - 128, 768), lambda i, s: (s[0], 0, 0)),
            pl.BlockSpec((2, own - 128, width), lambda i, s: (s[0], 0, 0)),
            pl.BlockSpec((1, 8, 2 * own), lambda i, s: (s[0], 0, 0)),
        ],
        scratch_shapes=[pltpu.VMEM((2, own, width), jnp.bfloat16)],
    )
    return pl.pallas_call(
        project_kernel,
        grid_spec=grid_spec,
        out_shape=shapes,
        input_output_aliases={4 + i: i for i in range(len(buffers))},
        compiler_params=params(20),
        cost_estimate=pl.CostEstimate(
            flops=4 * own * width * 768, bytes_accessed=4 * 2**20, transcendentals=0
        ),
        name="project",
    )(where, xa, xb, w, *buffers, *tokens)


def swap_pairs(values):
    lane = lax.broadcasted_iota(jnp.int32, values.shape, 1)
    after = pltpu.roll(values, values.shape[1] - 1, 1)
    before = pltpu.roll(values, 1, 1)
    return jnp.where(lane % 2 == 0, after, before)


def attend_kernel(
    prompt, starts, q, k, v, g0, g1, g2, g3, scales, gain, cosine, sine, cached_at, *refs
):
    out, key_out = refs[-2:]
    cached = [
        jnp.concatenate([g[r, kind, 0] for g in (g0, g1, g2, g3) for r in range(2)], axis=0)
        for kind in range(2)
    ]
    width = 8 * 256
    scale = lax.rsqrt(jnp.transpose(scales[0]) / width + EPSILON)
    cos_t, sin_t = cosine[0], sine[0]

    def turn(raw, which):
        val = raw[0].astype(jnp.float32) * scale[:, which : which + 1] * gain[which : which + 1, :]
        return (val * cos_t + swap_pairs(val) * sin_t).astype(jnp.bfloat16)

    queries = turn(q, 0)
    keys = turn(k, 1)
    key_out[0] = keys
    dims = (((1,), (1,)), ((), ()))
    factor = HD ** (-0.5)
    rows = queries.shape[0]
    old = lax.dot_general(queries, cached[0], dims, preferred_element_type=jnp.float32) * factor
    new = lax.dot_general(queries, keys, dims, preferred_element_type=jnp.float32) * factor
    live_old = cached_at[...] < starts[prompt]
    live_new = lax.broadcasted_iota(jnp.int32, (rows, rows), 1) <= lax.broadcasted_iota(
        jnp.int32, (rows, rows), 0
    )
    old = jnp.where(live_old, old, MASKED_SCORE)
    new = jnp.where(live_new, new, MASKED_SCORE)
    top = jnp.maximum(
        jnp.max(old, axis=1, keepdims=True), jnp.max(new, axis=1, keepdims=True)
    )
    old = jnp.exp(old - top)
    new = jnp.exp(new - top)
    total = jnp.sum(old, axis=1, keepdims=True) + jnp.sum(new, axis=1, keepdims=True)
    mixed = jnp.dot(old.astype(jnp.bfloat16), cached[1], preferred_element_type=jnp.float32)
    mixed = mixed + jnp.dot(new.astype(jnp.bfloat16), v[0], preferred_element_type=jnp.float32)
    out[0] = (mixed / total).astype(jnp.bfloat16)


def attend(prompt, starts, qkv, cached, scales, gain, cosine, sine, cached_at, buffers, tokens):
    group = qkv.shape[1]
    part = cached[0].shape[3]
    ctx = 8 * part
    head = lambda off: pl.BlockSpec((1, group, HD), lambda h, s: (prompt, 0, off + h))
    grid_spec = pltpu.PrefetchScalarGridSpec(
        num_scalar_prefetch=1,
        grid=(2,),
        in_specs=[
            head(0),
            head(2),
            head(4),
            *[pl.BlockSpec((2, 2, 1, part, HD), lambda h, s: (0, 0, prompt, 0, h))] * Z,
            pl.BlockSpec((1, 8, group), lambda h, s: (prompt, 0, 0)),
            pl.BlockSpec((2, HD), lambda h, s: (0, h)),
            pl.BlockSpec((1, group, HD), lambda h, s: (prompt, 0, 0)),
            pl.BlockSpec((1, group, HD), lambda h, s: (prompt, 0, 0)),
            pl.BlockSpec((1, ctx), lambda h, s: (0, 0)),
        ]
        + [ANY] * (len(buffers) + len(tokens)),
        out_specs=[head(0), head(0)],
    )
    made = jax.ShapeDtypeStruct((2, group, 2 * HD), jnp.bfloat16)
    return pl.pallas_call(
        functools.partial(attend_kernel, prompt),
        grid_spec=grid_spec,
        out_shape=[made, made],
        input_output_aliases={13 + i: i for i in range(len(buffers))},
        compiler_params=params(16),
        cost_estimate=pl.CostEstimate(
            flops=8 * group * (group + ctx) * HD,
            bytes_accessed=6 * 2**20,
            transcendentals=2 * group * (group + ctx),
        ),
        name="attend",
    )(starts, qkv, qkv, qkv, *cached, scales, gain, cosine, sine, cached_at, *buffers, *tokens)


def decode_kernel(lengths, q, gains, cosine, sine, *refs):
    caches = refs[:4]
    mixed, marks, queries = refs[4:]
    step = pl.program_id(0)
    heads = q.shape[1] // HD
    width = q.shape[1]
    ctx = caches[0].shape[2]
    count = 8

    @pl.when(step == 0)
    def _():
        val = q[...].astype(jnp.float32)
        val = val * lax.rsqrt(jnp.mean(val * val, axis=1, keepdims=True) + EPSILON)
        val = val * gains[0:1, :]
        cos_t = jnp.concatenate([cosine[...]] * heads, axis=1)
        sin_t = jnp.concatenate([sine[...]] * heads, axis=1)
        val = val * cos_t + swap_pairs(val) * sin_t
        queries[...] = val.astype(jnp.bfloat16).astype(jnp.float32)

    first = lengths[lengths.shape[0] - 1]
    shape = (heads, width)
    own_head = lax.broadcasted_iota(jnp.int32, shape, 1) // HD == lax.broadcasted_iota(
        jnp.int32, shape, 0
    )
    rows, limits = [], []
    for j in range(count):
        slot = step * count + j
        row = jnp.broadcast_to(queries[pl.ds(slot, 1), :], shape)
        rows.append(jnp.where(own_head, row, 0.0).astype(jnp.bfloat16))
        limits.append(jnp.broadcast_to(lengths[slot] - first, (heads, 1)))
    keys = jnp.concatenate([cache[0, j] for cache in caches for j in range(2)], axis=0)
    values = jnp.concatenate([cache[1, j] for cache in caches for j in range(2)], axis=0)
    scores = lax.dot_general(
        jnp.concatenate(rows, axis=0),
        keys,
        (((1,), (1,)), ((), ())),
        preferred_element_type=jnp.float32,
    ) * HD ** (-0.5)
    size = (count * heads, count * ctx)
    line = lax.broadcasted_iota(jnp.int32, size, 0) // heads
    at = lax.broadcasted_iota(jnp.int32, size, 1) - line * ctx
    live = (at >= 0) & (at < ctx) & (at < jnp.concatenate(limits, axis=0))
    scores = jnp.where(live, scores, MASKED_SCORE)
    top = jnp.max(scores, axis=1, keepdims=True)
    weights = jnp.where(live, jnp.exp(scores - top), 0.0)
    total = jnp.sum(weights, axis=1, keepdims=True)
    marks[0, :, 0:1] = top
    marks[0, :, 1:2] = total
    part = jnp.dot(weights.astype(jnp.bfloat16), values, preferred_element_type=jnp.float32)
    for j in range(count):
        mixed[j : j + 1, :] = jnp.sum(
            jnp.where(own_head, part[j * heads : (j + 1) * heads], 0.0), axis=0, keepdims=True
        )


def decode(lengths, q, gains, cosine, sine, cache, skip):
    slots, width = q.shape
    ctx = cache.shape[2]
    heads = width // HD
    steps = slots // 8
    whole = lambda shape: pl.BlockSpec(shape, lambda i, s: (0, 0))
    pair = lambda j: pl.BlockSpec(
        (2, 2, ctx, width), lambda i, s: (0, i * 4 + j + skip // 2, 0, 0)
    )
    grid_spec = pltpu.PrefetchScalarGridSpec(
        num_scalar_prefetch=1,
        grid=(steps,),
        in_specs=[
            whole(q.shape),
            whole(gains.shape),
            whole(cosine.shape),
            whole(sine.shape),
        ]
        + [pair(j) for j in range(4)],
        out_specs=[
            pl.BlockSpec((8, width), lambda i, s: (i, 0)),
            pl.BlockSpec((1, 8 * heads, 2), lambda i, s: (i, 0, 0)),
        ],
        scratch_shapes=[pltpu.VMEM(q.shape, jnp.float32)],
    )
    mixed, marks = pl.pallas_call(
        decode_kernel,
        grid_spec=grid_spec,
        out_shape=[
            jax.ShapeDtypeStruct((slots, width), jnp.float32),
            jax.ShapeDtypeStruct((steps, 8 * heads, 2), jnp.float32),
        ],
        compiler_params=params(52),
        cost_estimate=pl.CostEstimate(
            flops=4 * slots * 128 * ctx * width, bytes_accessed=13 * 2**20, transcendentals=0
        ),
        name="decode",
    )(lengths, q, gains, cosine, sine, cache, cache, cache, cache)
    marks = marks.reshape(slots, heads, 2)
    return mixed, marks[..., 0], marks[..., 1]


def assemble_kernel(core, own, other, out, sems):
    made = []
    for j in range(4):
        for k, part in enumerate((own, other)):
            col = pl.multiple_of(j * 512 + (core[0] ^ k) * 256, 256)
            made.append(
                pltpu.make_async_copy(
                    part.at[j], out.at[:, pl.ds(col, 256)], sems.at[2 * j + k]
                )
            )
    for copy in made:
        copy.start()
    for copy in made:
        copy.wait()


def assemble(core, own, other):
    rows = own.shape[1]
    return pl.pallas_call(
        assemble_kernel,
        in_specs=[SMEM, ANY, ANY],
        out_specs=ANY,
        out_shape=jax.ShapeDtypeStruct((rows, 8 * 256), jnp.bfloat16),
        scratch_shapes=[pltpu.SemaphoreType.DMA((8,))],
        compiler_params=params(4),
        cost_estimate=pl.CostEstimate(flops=0, bytes_accessed=17 * 2**20, transcendentals=0),
        name="assemble",
    )(core, own, other)


def mix_kernel(where, *refs):
    lines = refs[:8]
    att, w, dec, dec_x, gain, out, xs, sems = refs[8:]
    step = pl.program_id(0)
    core = where[Z]
    copies = [
        pltpu.make_async_copy(lines[i], xs.at[where[i // 2], core ^ (i % 2)], sems.at[i])
        for i in range(8)
    ]

    @pl.when(step == 0)
    def _():
        for copy in copies:
            copy.start()

    sides = []
    for c in range(2):
        for p in range(2):
            sides.append(
                jnp.concatenate([att[k, p, c * 64 : (c + 1) * 64] for k in range(8)], axis=1)
            )
        sides.append(dec[c])
    rows = jnp.concatenate(sides, axis=0)
    total = jnp.dot(rows, w[...], preferred_element_type=jnp.float32)

    @pl.when(step == 0)
    def _():
        for copy in copies:
            copy.wait()

    inv = lax.rsqrt(jnp.mean(total * total, axis=1, keepdims=True) + EPSILON)
    total = total * inv * gain[2:3, :]
    per = 128 + BLOCK_PAD
    for c in range(2):
        base = c * per
        out[c, :128] = (
            xs[step, c, :128].astype(jnp.float32) + total[base : base + 128]
        ).astype(jnp.bfloat16)
        out[c, 128:] = (
            dec_x[c].astype(jnp.float32) + total[base + 128 : base + per]
        ).astype(jnp.bfloat16)


def mix(where, lines, att, w, dec, dec_x, gains):
    width = w.shape[1]
    return pl.pallas_call(
        mix_kernel,
        grid=(Z,),
        in_specs=[SMEM]
        + [ANY] * 8
        + [
            pl.BlockSpec((8, 2, 128, 256), lambda i: (0, 0, i, 0)),
            VMEM,
            pl.BlockSpec((2, BLOCK_PAD, width), lambda i: (i, 0, 0)),
            pl.BlockSpec((2, BLOCK_PAD, width), lambda i: (i, 0, 0)),
            pl.BlockSpec(gains.shape, lambda i: (0, 0)),
        ],
        out_specs=pl.BlockSpec((2, 128 + BLOCK_PAD, width), lambda i: (i, 0, 0)),
        out_shape=jax.ShapeDtypeStruct((8, 128 + BLOCK_PAD, width), jnp.bfloat16),
        scratch_shapes=[
            pltpu.VMEM((Z, 2) + lines[0].shape, jnp.bfloat16),
            pltpu.SemaphoreType.DMA((8,)),
        ],
        compiler_params=params(18),
        cost_estimate=pl.CostEstimate(
            flops=2 * 8 * 144 * width * width, bytes_accessed=22 * 2**20, transcendentals=0
        ),
        name="mix",
    )(where, *lines, att, w, dec, dec_x, gains)


def deliver_kernel(where, a, b, c, d, prompt_out, decode_out):
    for k, part in enumerate((a, b, c, d)):
        for r in range(2):
            cols = pl.ds(pl.multiple_of(where[2 * k + r] * 256, 256), 256)
            for kind in range(2):
                block = part[r, kind]
                prompt_out[kind, :, cols] = block[:128]
                decode_out[kind, :, cols] = block[128:]


def deliver(where, came, width):
    own = came[0].shape[2]
    return pl.pallas_call(
        deliver_kernel,
        in_specs=[SMEM] + [VMEM] * 4,
        out_specs=[VMEM, VMEM],
        out_shape=[
            jax.ShapeDtypeStruct((2, 128, width), jnp.bfloat16),
            jax.ShapeDtypeStruct((2, own - 128, width), jnp.bfloat16),
        ],
        compiler_params=params(8),
        cost_estimate=pl.CostEstimate(flops=0, bytes_accessed=2**22, transcendentals=0),
        name="deliver",
    )(where, *came)


def forward_kernel(where, hidden, wgu, wd, *refs):
    mine, other, acc = refs[-3:]
    per = hidden.shape[1]
    rows = hidden[pl.ds(where[0] * 2, 2)].reshape(2 * per, hidden.shape[2])
    half = wd.shape[0] // 2
    total = None
    for i in range(2):
        cols = pl.ds(i * half, half)
        gate = jnp.dot(rows, wgu[0, :, cols], preferred_element_type=jnp.float32)
        up = jnp.dot(rows, wgu[1, :, cols], preferred_element_type=jnp.float32)
        act = (gate / (1.0 + jnp.exp(-gate)) * up).astype(jnp.bfloat16)
        part = jnp.dot(act, wd[cols], preferred_element_type=jnp.float32)
        total = part if total is None else total + part
    acc[...] = total.reshape(acc.shape)
    core = where[1]
    mine[...] = acc[core, : mine.shape[0]].astype(jnp.bfloat16)
    other[...] = acc[1 - core, : mine.shape[0]].astype(jnp.bfloat16)


def forward(where, hidden, wgu, wd, rows, tokens):
    per, width = hidden.shape[1:]
    made = jax.ShapeDtypeStruct((rows, width), jnp.bfloat16)
    return pl.pallas_call(
        forward_kernel,
        in_specs=[SMEM, VMEM, VMEM, VMEM] + [ANY] * len(tokens),
        out_specs=[VMEM, VMEM],
        out_shape=[made, made],
        scratch_shapes=[pltpu.VMEM((2, per, width), jnp.float32)],
        compiler_params=params(12),
        cost_estimate=pl.CostEstimate(
            flops=12 * per * width * wd.shape[0], bytes_accessed=4 * 2**20, transcendentals=0
        ),
        name="forward",
    )(where, hidden, wgu, wd, *tokens)


def tables(positions):
    lanes = jnp.arange(HD, dtype=jnp.int32)
    freq_index = (lanes // 2).astype(jnp.float32)
    inv_freq = jnp.power(ROPE_BASE, -2.0 * freq_index / HD)
    angles = positions.astype(jnp.float32)[..., None] * inv_freq
    sign = jnp.where(lanes % 2 == 0, -1.0, 1.0)
    return jnp.cos(angles), jnp.sin(angles) * sign


def turn_kernel(where, a, b, up, down, up_out, down_out):
    chip = where[0]
    one, two = a[...].astype(jnp.float32), b[...].astype(jnp.float32)
    up_out[...] = (jnp.where(chip == 1, one, two) + up[...]).astype(jnp.bfloat16)
    down_out[...] = (jnp.where(chip == 2, one, two) + down[...]).astype(jnp.bfloat16)


def turn_sums(where, a, b, up, down):
    made = jax.ShapeDtypeStruct(a.shape, a.dtype)
    return pl.pallas_call(
        turn_kernel,
        in_specs=[SMEM] + [VMEM] * 4,
        out_specs=[VMEM, VMEM],
        out_shape=[made, made],
        compiler_params=params(10),
        cost_estimate=pl.CostEstimate(flops=0, bytes_accessed=2**22, transcendentals=0),
        name="turn_sums",
    )(where, a, b, up, down)


def narrow_sum(*terms):
    total = terms[0].astype(jnp.float32)
    for term in terms[1:]:
        total = total + term.astype(jnp.float32)
    return total.astype(jnp.bfloat16)


def after(values, *others):
    return lax.optimization_barrier((values,) + others)[0]


def local_heads(
    prompt_states,
    decode_states,
    cache,
    prompt_starts,
    decode_lengths,
    decode_slots,
    w_qkv,
    w_out,
    w_gate_up,
    w_down,
    gains,
):
    place = lax.axis_index("tensor")
    chip, core = place // 2, place % 2
    data_pos = lax.axis_index("dp")
    pre_dev, part_rows, width = prompt_states.shape
    dec_part = decode_states.shape[0]
    group = part_rows * 8
    dec_dev = dec_part * 8
    ctx_part = cache.shape[2]
    heads = width // HD
    own_rows = pre_dev * part_rows + dec_part
    states = jnp.concatenate(
        [prompt_states.reshape(pre_dev * part_rows, width), decode_states], axis=0
    )
    starts = lax.dynamic_slice_in_dim(prompt_starts, data_pos * pre_dev, pre_dev)
    slot_ids = data_pos * dec_dev + jnp.arange(dec_dev, dtype=jnp.int32)
    matches = decode_slots[None, :] == slot_ids[:, None]
    slot_length = jnp.sum(jnp.where(matches, decode_lengths[None, :], 0), axis=1)
    prompt_pos = starts[:, None] + jnp.arange(group, dtype=jnp.int32)[None, :]
    cos_p, sin_p = tables(prompt_pos)
    cos_d, sin_d = tables(slot_length)
    my_gains = lax.dynamic_slice_in_dim(gains[:2], place * 256, 256, 1)

    chips_at = (chip - jnp.arange(Z, dtype=jnp.int32)) % Z
    blocks_at = jnp.stack([chips_at * 2 + core, chips_at * 2 + 1 - core], axis=1).astype(jnp.int32)
    low, end = chip < 2, (chip == 0) | (chip == Z - 1)

    lines = []

    def add_block(line, source, buffers, *tokens):
        at = jnp.stack([source, core]).astype(jnp.int32)
        other = send(line, CORE)
        lines.extend([line, other])
        return project(at, line, other, w_qkv, buffers, tokens)

    rise1, fall1 = send(states, UP[0]), send(states, DOWN[0])
    prompt_cache = cache[:, :pre_dev]
    prompt_cache = jnp.stack(
        [
            jnp.stack(
                [prompt_cache[..., (2 * z + c) * 256 : (2 * z + c + 1) * 256] for c in range(2)]
            )
            for z in range(Z)
        ]
    )
    cache_pair = swap_cores(prompt_cache, core)
    buffers = add_block(states, chip, (), cache_pair)
    rise2, fall2 = send(rise1, UP[1]), send(fall1, DOWN[1])
    line = jnp.where(chip % 2 == 0, fall1, rise1)
    buffers = add_block(line, chip ^ 1, buffers)
    stats_early = buffers[3]
    rise2, fall2, *buffers = lax.optimization_barrier((rise2, fall2, *buffers))
    rise3, fall3 = send(rise2, UP[2]), send(fall2, DOWN[2])
    line = jnp.where(low, jnp.where(end, fall2, fall1), jnp.where(end, rise2, rise1))
    buffers = add_block(line, jnp.where(low, 2, 1), buffers)
    rise3, fall3, *buffers = lax.optimization_barrier((rise3, fall3, *buffers))
    line = jnp.where(low, jnp.where(end, fall3, fall2), jnp.where(end, rise3, rise2))
    buffers = add_block(line, jnp.where(low, 3, 0), buffers)
    prompt_raw, decode_raw, dec_x, stats = buffers
    prompt_raw = prompt_raw.reshape(pre_dev, group, 768)
    decode_raw = decode_raw.reshape(dec_dev, 768)

    cached_at = (
        blocks_at.reshape(8, 1) * ctx_part + jnp.arange(ctx_part, dtype=jnp.int32)[None, :]
    ).reshape(1, 8 * ctx_part)

    share = width // 4
    w_share = lax.dynamic_slice_in_dim(w_out, data_pos * share, share, 1)
    w_share = w_share.reshape(1, w_out.shape[0], 2, share // 2)
    w_pair = swap_cores(jnp.transpose(w_share, (0, 2, 1, 3)), core)[0]
    w_pair = jnp.where(core == 0, w_pair, w_pair[::-1])
    lanes = [[2 * z + c for z in range(Z)] for c in range(2)]
    w_line = lax.all_gather(w_pair, "tensor", axis=0, axis_index_groups=lanes)
    w_line = hold(w_line, stats_early)
    w_own = lax.all_gather(w_line.reshape(width, share // 2), "dp", axis=0)
    w_full = assemble(core[None].astype(jnp.int32), w_own, send(w_own, CORE))

    stats = small_sum(stats).reshape(Z, 8, 2, own_rows)
    prompt_stats = stats[..., : own_rows - dec_part].reshape(Z, 8, 2, pre_dev, part_rows)
    prompt_stats = jnp.transpose(prompt_stats, (3, 1, 0, 2, 4)).reshape(pre_dev, 8, group)
    dec_stats = jnp.transpose(stats[..., own_rows - dec_part :], (0, 2, 3, 1)).reshape(dec_dev, 8)
    dec_scales = lax.rsqrt(dec_stats / width + EPSILON)
    def turn(raw, scale, gain):
        val = raw.astype(jnp.float32) * scale * gain
        even = jnp.arange(val.shape[1]) % 2 == 0
        swapped = jnp.where(even, jnp.roll(val, -1, axis=1), jnp.roll(val, 1, axis=1))
        cos_t = jnp.concatenate([cos_d] * 2, axis=1)
        sin_t = jnp.concatenate([sin_d] * 2, axis=1)
        return (val * cos_t + swapped * sin_t).astype(jnp.bfloat16).reshape(-1, 2, HD)

    query_mine = turn(decode_raw[:, :256], dec_scales[:, :1], my_gains[0])
    key_mine = turn(decode_raw[:, 256:512], dec_scales[:, 1:2], my_gains[1])
    value_mine = decode_raw[:, 512:].reshape(dec_dev, 2, HD)
    query_all = small_gather(decode_raw[:, :256], chip, core)
    query_all = jnp.swapaxes(query_all, 0, 1).reshape(dec_dev, width)
    got = spread_chips(hold(cache_pair, query_all), chip)
    scale_factor = HD ** (-0.5)
    lengths = jnp.concatenate([slot_length, (place * ctx_part)[None]]).astype(jnp.int32)
    mixed, tops, sums = decode(lengths, query_all, gains, cos_d, sin_d, cache, pre_dev)
    parts = jnp.concatenate(
        [
            jnp.transpose(mixed.reshape(dec_dev, 8, 256), (1, 0, 2)),
            jnp.transpose(tops.reshape(dec_dev, 8, 2), (1, 0, 2)),
            jnp.transpose(sums.reshape(dec_dev, 8, 2), (1, 0, 2)),
        ],
        axis=-1,
    )
    parts = swap_cores(parts.reshape(Z, 2, dec_dev, 260), core)
    arrived = spread_chips(parts, chip)
    made = ()
    for prompt, tokens in enumerate(((parts,), arrived)):
        made = attend(
            prompt,
            starts,
            prompt_raw,
            got,
            prompt_stats,
            my_gains,
            cos_p,
            sin_p,
            cached_at,
            made,
            tokens,
        )
    attended, key_new = made
    arrived = jnp.stack(arrived).reshape(8, dec_dev, 260)
    got_mixed = arrived[..., :256].reshape(8, dec_dev, 2, HD)
    got_tops, got_sums = arrived[..., 256:258], arrived[..., 258:]
    own_score = (
        jnp.sum(query_mine.astype(jnp.float32) * key_mine.astype(jnp.float32), axis=-1)
        * scale_factor
    )
    highest = jnp.maximum(jnp.max(got_tops, axis=0), own_score)
    factors = jnp.exp(got_tops - highest[None])
    own_weight = jnp.exp(own_score - highest)
    total = jnp.sum(got_sums * factors, axis=0) + own_weight
    summed = jnp.sum(got_mixed * factors[..., None], axis=0)
    summed = summed + own_weight.astype(jnp.bfloat16).astype(jnp.float32)[
        ..., None
    ] * value_mine.astype(jnp.float32)
    dec_attended = (summed / total[..., None]).reshape(dec_dev, 256).astype(jnp.bfloat16)
    wanted = lax.dynamic_slice_in_dim(decode_slots, data_pos * dec_dev, dec_dev)
    by_request = jnp.take(
        data_gather(dec_attended, data_pos).reshape(4 * dec_dev, 256), wanted, axis=0
    )
    pad = lambda v: jnp.pad(
        v.reshape(8, dec_part, width), ((0, 0), (0, BLOCK_PAD - dec_part), (0, 0))
    )
    dec_rows = small_gather(by_request, chip, core)
    dec_rows = pad(jnp.swapaxes(dec_rows, 0, 1).reshape(dec_dev, width))
    dec_x = after(dec_x.reshape(dec_dev, width), attended)
    dec_x = data_gather(dec_x, data_pos)
    dec_x = pad(jnp.take(dec_x.reshape(4 * dec_dev, width), wanted, axis=0))

    fresh = jnp.stack([key_new, prompt_raw[:, :, 512:]])
    fresh = fresh.reshape(2, pre_dev, 8, part_rows, 256)
    fresh = jnp.transpose(fresh, (2, 0, 1, 3, 4)).reshape(8, 2, pre_dev * part_rows, 256)
    fresh_dec = jnp.stack([key_mine.reshape(dec_dev, 256), decode_raw[:, 512:]])
    fresh_dec = jnp.transpose(fresh_dec.reshape(2, 8, dec_part, 256), (1, 0, 2, 3))
    fresh = jnp.concatenate([fresh, fresh_dec], axis=2)
    fresh_pair = swap_cores(fresh.reshape(Z, 2, 2, own_rows, 256), core)

    att = lax.all_gather(attended, "tensor", axis=0)
    fresh_pair = after(fresh_pair, att)
    kv_came = spread_chips(fresh_pair, chip)
    where = jnp.stack(
        [chip, chip ^ 1, jnp.where(low, 2, 1), jnp.where(low, 3, 0), core]
    ).astype(jnp.int32)
    hidden = mix(where, lines, att, w_full, dec_rows, dec_x, gains)

    orders = jnp.array([[3, 2, 1, 0], [3, 2, 0, 1], [0, 1, 3, 2], [0, 1, 2, 3]], jnp.int32)
    order = lax.dynamic_index_in_dim(orders, chip, 0, keepdims=False)
    sums = []
    for k in range(Z):
        at = jnp.stack([order[k], core]).astype(jnp.int32)
        tokens = [kv_came, sums, (), ()][k]
        mine, other = forward(at, hidden, w_gate_up, w_down, own_rows, tokens)
        sums.append(narrow_sum(mine, send(other, CORE)))
    came = after(send(sums[0], ENDS), mine)
    is_end = (chip == 0) | (chip == 3)
    load = narrow_sum(jnp.where(is_end, sums[1], sums[0]), came)
    up, down = send(load, RISE[0]), send(load, FALL[0])
    up, down = turn_sums(chip[None].astype(jnp.int32), sums[1], sums[2], up, down)
    up, down = send(up, RISE[1]), send(down, FALL[1])
    ffn_sum = sums[3].astype(jnp.float32) + up.astype(jnp.float32) + down.astype(jnp.float32)
    hidden_own = lax.dynamic_index_in_dim(hidden, place, 0, keepdims=False)[:own_rows]
    output = (hidden_own.astype(jnp.float32) + rms_scale(ffn_sum, gains[3])).astype(jnp.bfloat16)
    prompt_out = output[: own_rows - dec_part].reshape(pre_dev, part_rows, width)
    decode_out = output[own_rows - dec_part :]

    new_prompt_kv, new_decode_kv = deliver(blocks_at.reshape(8), kv_came, width)
    new_prompt_kv = new_prompt_kv.reshape(2, pre_dev, part_rows, width)
    return (prompt_out, decode_out, new_prompt_kv, new_decode_kv)


def fits_heads(mesh):
    return mesh.shape["tensor"] == 2 * Z and mesh.shape["dp"] == 4


def solution(mesh):
    in_specs = (
        P("dp", "tensor", None),
        P(("dp", "tensor"), None),
        P(None, "dp", "tensor", None),
        P(),
        P(),
        P(),
        P(None, None, "tensor"),
        P("tensor", None),
        P(None, None, "tensor"),
        P("tensor", None),
        P(),
    )
    out_specs = (
        P("dp", "tensor", None),
        P(("dp", "tensor"), None),
        P(None, "dp", "tensor", None),
        P(None, ("dp", "tensor"), None),
    )
    body = local_heads if fits_heads(mesh) else local
    return jax.shard_map(body, mesh=mesh, in_specs=in_specs, out_specs=out_specs, check_vma=False)
```
